32 devices in a mesh: tm: 4 (over y, x), sta: 8 (over z, core).
Axes of the slice: x: 2, y: 2, z: 4, core: 2. Of those that a mesh axis runs over, the one named last changes fastest.
Arguments:
- templates: bfloat16 [4, 256, 8, 3, 600], P('tm', None, 'sta'), may hold values from -6 to 6
- channel_mask: int32 [4, 256, 8], P('tm', None, 'sta'), may hold values 0 or 1
- waveforms: bfloat16 [8, 3, 3584], P('sta', None, 'tm'), may hold values from -60 to 60
- waveform_tail: bfloat16 [8, 3, 599], P('sta'), may hold values from -6 to 6
Outputs:
- detections: float32 [4, 256, 3584], P(None, 'sta', 'tm')
The draws below stay inside these ranges and needn't reach their ends.
All inputs are finite; a program needn't handle non-finite values. No bound on the sum of `channel_mask` on one device may be relied on, other than what follows from the above.
Results may differ from the reference program's by a relative error of at most 0.0044.
Values may be sent and summed in bfloat16 or wider, within the bound.
No kernel may reach another device: no remote copies, remote signals or barrier semaphores. Data moves between devices by JAX's collectives and lax.ppermute only.
A program may use at most 128 MiB of HBM per device.

```python
import math
import jax
import jax.numpy as jnp
from jax import lax

L = 600
TPL_DEV = 256
TBLOCKS = 4
TEMPLATES = 1024
STATIONS = 8
SAMPLES = 3584
HALO = 599


def draw_waveforms(key, part):
    noise_key = jax.random.fold_in(key, 11)
    level_key = jax.random.fold_in(key, 12)
    array_shape = (STATIONS, 3, SAMPLES)
    noise = jax.random.truncated_normal(noise_key, -6.0, 6.0, array_shape, jnp.float32)
    levels = jax.random.uniform(level_key, (STATIONS, 3, SAMPLES // 64, 1), jnp.float32, 0.0, math.log(10.0))
    envelope = jnp.broadcast_to(jnp.exp(levels), (STATIONS, 3, SAMPLES // 64, 64)).reshape(array_shape)
    return (noise * envelope).astype(jnp.bfloat16)


def set_ends(result, own_key, smallest, top_value):
    extent = result.shape
    spot = [jax.random.randint(jax.random.fold_in(own_key, axis), (), 0, extent[axis]) for axis in range(len(extent))]
    result = result.at[tuple(spot)].set(smallest)
    longest = extent.index(max(extent))
    spot[longest] = (spot[longest] + 1) % extent[longest]
    return result.at[tuple(spot)].set(top_value)


def with_spikes(result, stream_key, source, target, parts, factor):
    def block_of(axis_at):
        return (jnp.arange(result.shape[axis_at]) // (result.shape[axis_at] // parts)).reshape((-1,) + (1,) * (result.ndim - 1 - axis_at))

    first = jax.random.permutation(stream_key, parts)[block_of(target)]
    second = (block_of(target) + parts // 2) % parts
    return jnp.where((block_of(source) == first) | (block_of(source) == second), factor * result, result)


def shard_levels(own_key, dims, cuts, least, largest):
    gain = 1.0
    for dim, blocks in cuts:
        steps = jax.random.uniform(jax.random.fold_in(jax.random.fold_in(own_key, 6), dim), (blocks,), jnp.float32, least / len(cuts), largest / len(cuts))
        gain = gain * jnp.repeat(jnp.exp(steps), dims[dim] // blocks).reshape((-1,) + (1,) * (len(dims) - 1 - dim))
    return gain


def scatter_about(rng, shape, scale, most, cuts=(), dtype=jnp.bfloat16):
    factor_of = shard_levels(rng, shape, cuts, -0.22, 0.18) if cuts else 1.0
    values = jax.random.normal(rng, shape, jnp.float32) * scale * factor_of
    return jnp.minimum(jnp.maximum(values, -most), most).astype(dtype)


def bell_draw_with(stream_key, extent, deviation, most, split, heavy, held_as=jnp.bfloat16):
    entries = deviation * jax.random.normal(stream_key, extent, jnp.float32)
    if split:
        entries = entries * shard_levels(stream_key, extent, split, -0.22, 0.18)
    return jnp.clip(with_spikes(entries, jax.random.fold_in(stream_key, 3), *heavy), -most, most).astype(held_as)


def setup_inputs(seed: int = 0) -> dict:
    arg_keys = jax.random.split(jax.random.key(seed), 5)
    return {
        "templates": bell_draw_with(arg_keys[0], (TBLOCKS, TPL_DEV, STATIONS, 3, L), 1.0, 6.0, ((0, 4), (2, 8)), (2, 1, 8, 2.0)),
        "channel_mask": set_ends((jax.random.randint(arg_keys[1], (TBLOCKS, TPL_DEV, STATIONS), 0, 4) < 3).astype(jnp.int32), jax.random.fold_in(arg_keys[1], 1), 0, 1),
        "waveforms": draw_waveforms(jax.random.fold_in(arg_keys[4], 71), 0),
        "waveform_tail": scatter_about(arg_keys[3], (STATIONS, 3, HALO), 1.0, 6.0, ((0, 8),)),
    }


def normalize(templates, channel_mask):
    values = templates.astype(jnp.float32)
    centred = values - lax.optimization_barrier(jnp.mean(values, axis=-1, keepdims=True))
    energy = lax.optimization_barrier(jnp.sum(centred * centred, axis=-1, keepdims=True))
    weighted = centred * lax.rsqrt(energy + 1e-05) * channel_mask.astype(jnp.float32)[..., None, None]
    return weighted.astype(jnp.bfloat16)

def windows(extended, length, sample_count):
    values = extended.astype(jnp.float32)
    zero_col = jnp.zeros(values.shape[:-1] + (1,), jnp.float32)
    prefix_one = jnp.concatenate([zero_col, jnp.cumsum(values, axis=-1)], axis=-1)
    prefix_two = jnp.concatenate([zero_col, jnp.cumsum(values * values, axis=-1)], axis=-1)
    window_sum = prefix_one[..., length:length + sample_count] - prefix_one[..., :sample_count]
    window_square = prefix_two[..., length:length + sample_count] - prefix_two[..., :sample_count]
    inverse = lax.rsqrt(window_square - window_sum * window_sum / length + 1e-05)
    span = extended.shape[-1]
    leading = extended.shape[:-1]
    copies = jnp.broadcast_to(extended[..., None, :], leading + (length + 1, span))
    flat = copies.reshape(leading + ((length + 1) * span,))
    hankel = flat[..., :length * (span + 1)].reshape(leading + (length, span + 1))[..., :sample_count]
    return (hankel.astype(jnp.float32) * inverse[..., None, :]).astype(jnp.bfloat16)

def reference(templates, channel_mask, waveforms, waveform_tail):
    normed = normalize(templates, channel_mask)
    tpl_flat = normed.reshape(TEMPLATES, STATIONS, 3 * L)
    moved = jnp.moveaxis(tpl_flat, 1, 0)
    extended = jnp.concatenate([waveforms, waveform_tail], axis=-1)

    def station(total, pieces):
        station_tpl, station_wave = pieces
        scaled = windows(station_wave, L, SAMPLES).reshape(3 * L, SAMPLES)
        return (total + jnp.dot(station_tpl, scaled, preferred_element_type=jnp.float32), None)
    start_total = jnp.zeros((TEMPLATES, SAMPLES), jnp.float32)
    total, unused = lax.scan(station, start_total, (moved, extended))
    return total.reshape(TBLOCKS, TPL_DEV, SAMPLES)
```

```python
import functools
import jax
import jax.numpy as jnp
from jax import lax
from jax.experimental import pallas as pl
from jax.experimental.pallas import tpu as pltpu
from jax.sharding import PartitionSpec as P

F32 = jnp.float32
BF16 = jnp.bfloat16
LANES = 128
VMEM = pl.BlockSpec(memory_space=pltpu.VMEM)
SMEM = pl.BlockSpec(memory_space=pltpu.SMEM)


def params(limit_mib):
    return pltpu.CompilerParams(vmem_limit_bytes=limit_mib << 20)


def up(value, multiple):
    return (value + multiple - 1) // multiple * multiple


def swap_with(x, axis, offset):
    size = lax.axis_size(axis)
    return lax.ppermute(x, axis, [(i, i ^ offset) for i in range(size)])


def pack_kernel(chips, rows, length, place_ref, tpl_ref, mask_ref, wave_ref, tail_ref, *out_refs):
    tpl_outs, wave_out = out_refs[:chips], out_refs[chips]
    folds = LANES // rows
    fold_lags = tpl_outs[0].shape[1]
    samples = wave_ref.shape[-1]
    wave_out[...] = jnp.zeros_like(wave_out)
    wave_out[:, :samples] = wave_ref[...]
    wave_out[:, samples : samples + tail_ref.shape[-1]] = tail_ref[...]
    lane = lax.broadcasted_iota(jnp.int32, (1, LANES), 1)
    for offset in range(chips):
        target = place_ref[0] ^ offset
        tile = pl.multiple_of((target * rows) // LANES * LANES, LANES)
        start = (target * rows) % LANES
        mask = mask_ref[:, pl.ds(tile, LANES)].astype(F32)
        for comp in range(tpl_ref.shape[0]):
            values = tpl_ref[comp, :, pl.ds(tile, LANES)].astype(F32) * mask
            folded = jnp.zeros((fold_lags, LANES), F32)
            for fold in range(folds):
                piece = values[fold * fold_lags : min((fold + 1) * fold_lags, length)]
                if piece.shape[0] == 0:
                    continue
                if piece.shape[0] < fold_lags:
                    piece = jnp.concatenate(
                        [piece, jnp.zeros((fold_lags - piece.shape[0], LANES), F32)], axis=0
                    )
                turned = pltpu.roll(piece, (fold * rows - start + LANES) % LANES, 1)
                here = (lane >= fold * rows) & (lane < (fold + 1) * rows)
                folded = jnp.where(here, turned, folded)
            tpl_outs[offset][comp] = folded.astype(BF16)


def pack(place, tpl, mask, wave, tail, chips):
    comps, length, all_rows = tpl.shape
    rows = all_rows // chips
    fold_lags = up(-(-length // (LANES // rows)), 16)
    shapes = [jax.ShapeDtypeStruct((comps, fold_lags, LANES), BF16)] * chips
    shapes.append(jax.ShapeDtypeStruct((comps, up(wave.shape[-1] + tail.shape[-1], LANES)), BF16))
    return pl.pallas_call(
        functools.partial(pack_kernel, chips, rows, length),
        out_shape=shapes,
        in_specs=[SMEM] + [VMEM] * 4,
        out_specs=[VMEM] * len(shapes),
        compiler_params=params(16),
    )(place, tpl, mask, wave, tail)


def wave_kernel(shards, chips, length, halo, place_ref, *refs):
    shard_refs, tail_refs = refs[:shards], refs[shards : shards + chips]
    ext_ref, inv_ref = refs[shards + chips :]
    comps, samples = shard_refs[0].shape[1:]
    total = inv_ref.shape[-1]
    width = ext_ref.shape[-1]
    ext_ref[...] = jnp.zeros_like(ext_ref)
    for chip in range(chips):
        for offset in range(shards):
            at = pl.multiple_of((place_ref[1] ^ offset) * samples, LANES)
            ext_ref[chip * comps : (chip + 1) * comps, pl.ds(at, samples)] = shard_refs[offset][chip].astype(F32)
        ext_ref[chip * comps : (chip + 1) * comps, total : total + halo] = tail_refs[chip][
            :, samples : samples + halo
        ].astype(F32)

    def window(values):
        result, done, span, doubled = None, 0, 1, values
        while span <= length:
            if length & span:
                part = doubled if done == 0 else pltpu.roll(doubled, width - done, 1)
                result = part if result is None else result + part
                done += span
            span *= 2
            if span <= length:
                doubled = doubled + pltpu.roll(doubled, width - span // 2, 1)
        return result[:, :total]

    values = ext_ref[...]
    window_sum = window(values)
    window_square = window(values * values)
    inv_ref[...] = lax.rsqrt(window_square - window_sum * window_sum / length + 1e-05)


def wave_windows(place, shards, tails, length, halo):
    chips, comps, samples = shards[0].shape
    total = samples * len(shards)
    width = total + up(length, LANES)
    return pl.pallas_call(
        functools.partial(wave_kernel, len(shards), chips, length, halo),
        out_shape=[
            jax.ShapeDtypeStruct((chips * comps, width), F32),
            jax.ShapeDtypeStruct((chips * comps, total), F32),
        ],
        in_specs=[SMEM] + [VMEM] * (len(shards) + chips),
        out_specs=[VMEM] * 2,
        compiler_params=params(24),
    )(place, *shards, *tails)


def normed_rows(values, rows, length):
    fold_lags = values.shape[0]
    folds = LANES // rows

    def over_folds(total):
        span = rows
        while span < LANES:
            total = total + pltpu.roll(total, span, 1)
            span *= 2
        return total

    lane = lax.broadcasted_iota(jnp.int32, values.shape, 1)
    lag = lax.broadcasted_iota(jnp.int32, values.shape, 0) + lane // rows * fold_lags
    mean = over_folds(jnp.sum(values, axis=0, keepdims=True)) / length
    centred = jnp.where(lag < length, values - mean, 0.0)
    energy = over_folds(jnp.sum(centred * centred, axis=0, keepdims=True))
    weighted = centred * lax.rsqrt(energy + 1e-05)
    parts = [weighted] + [pltpu.roll(weighted, LANES - fold * rows, 1) for fold in range(1, folds)]
    return jnp.concatenate(parts, axis=0)


def piece_kernel(index, rows, length, tpl_ref, ext_ref, inv_ref, *refs):
    acc_ref, (out_ref, lags_ref, hankel_ref) = (refs[0] if len(refs) == 4 else None), refs[-3:]
    comps = tpl_ref.shape[0]
    width, total = ext_ref.shape[-1], inv_ref.shape[-1]
    blocks = up(-(-length // LANES), 2)
    flip = (
        lax.broadcasted_iota(jnp.int32, (LANES, LANES), 0)
        + lax.broadcasted_iota(jnp.int32, (LANES, LANES), 1)
        == LANES - 1
    ).astype(BF16)
    for comp in range(comps):
        spread = normed_rows(tpl_ref[comp].astype(F32), rows, length)[: blocks * LANES].astype(BF16)
        if spread.shape[0] < blocks * LANES:
            lags_ref[spread.shape[0] :, :] = jnp.zeros((blocks * LANES - spread.shape[0], LANES), BF16)
        lags_ref[: spread.shape[0], :] = spread
        turned = [
            lax.dot_general(
                lags_ref[block * LANES : (block + 1) * LANES, :],
                flip,
                (((0,), (0,)), ((), ())),
                preferred_element_type=F32,
            )[:rows].astype(BF16)
            for block in range(blocks)
        ]
        lhs = jnp.concatenate(
            [jnp.concatenate(turned[block : block + 2], axis=1) for block in range(0, blocks, 2)], axis=0
        )
        at = index * comps + comp
        row = jnp.broadcast_to(ext_ref[at : at + 1, :].astype(BF16), (LANES, width))
        hankel_ref[:, :width] = pltpu.roll(row, width - (LANES - 1), 1, stride=1, stride_axis=0)
        reach = total + (blocks - 2) * LANES
        rhs = jnp.concatenate([hankel_ref[:, :reach], hankel_ref[:, LANES : LANES + reach]], axis=0)
        product = jnp.dot(lhs, rhs, preferred_element_type=F32)
        gathered = product[:rows, :total]
        for split in range(1, blocks // 2):
            shift = split * 2 * LANES
            gathered = gathered + product[split * rows : (split + 1) * rows, shift : shift + total]
        gathered = gathered * inv_ref[at : at + 1, :]
        if comp == 0 and acc_ref is None:
            out_ref[...] = gathered
        elif comp == 0:
            out_ref[...] = acc_ref[...] + gathered
        else:
            out_ref[...] += gathered


def piece(index, rows, length, tpl, ext, inv, acc):
    total, width = inv.shape[-1], ext.shape[-1]
    blocks = up(-(-length // LANES), 2)
    inputs = [tpl, ext, inv] + ([] if acc is None else [acc])
    return pl.pallas_call(
        functools.partial(piece_kernel, index, rows, length),
        out_shape=jax.ShapeDtypeStruct((rows, total), F32),
        in_specs=[VMEM] * len(inputs),
        out_specs=VMEM,
        scratch_shapes=[
            pltpu.VMEM((blocks * LANES, LANES), BF16),
            pltpu.VMEM((LANES, up(width, LANES) + LANES), BF16),
        ],
        compiler_params=params(32),
        cost_estimate=pl.CostEstimate(
            flops=2 * rows * total * length * tpl.shape[0] * 3, bytes_accessed=tpl.size * 2, transcendentals=0
        ),
    )(*inputs)


def split_kernel(place_ref, acc_ref, keep_ref, send_ref):
    own = keep_ref.shape[0]
    at = pl.multiple_of(place_ref[2] * own, own)
    other = pl.multiple_of((1 - place_ref[2]) * own, own)
    keep_ref[...] = acc_ref[pl.ds(at, own), :]
    send_ref[...] = acc_ref[pl.ds(other, own), :].astype(BF16)


def split(place, acc):
    rows, total = acc.shape
    return pl.pallas_call(
        split_kernel,
        out_shape=[jax.ShapeDtypeStruct((rows // 2, total), F32), jax.ShapeDtypeStruct((rows // 2, total), BF16)],
        in_specs=[SMEM, VMEM],
        out_specs=[VMEM] * 2,
        compiler_params=params(16),
    )(place, acc)


def shard_kernel(place_ref, keep_ref, came_ref, own_ref, *send_refs):
    samples = own_ref.shape[-1]
    for offset, ref in enumerate((own_ref,) + send_refs):
        at = pl.multiple_of((place_ref[1] ^ offset) * samples, LANES)
        total = keep_ref[:, pl.ds(at, samples)] + came_ref[:, pl.ds(at, samples)].astype(F32)
        ref[...] = total.astype(ref.dtype)


def shard(place, keep, came, count):
    own, total = keep.shape
    samples = total // count
    return pl.pallas_call(
        shard_kernel,
        out_shape=[jax.ShapeDtypeStruct((own, samples), F32)]
        + [jax.ShapeDtypeStruct((own, samples), BF16)] * (count - 1),
        in_specs=[SMEM, VMEM, VMEM],
        out_specs=[VMEM] * count,
        compiler_params=params(16),
    )(place, keep, came)


def gather_kernel(place_ref, *refs):
    out_ref = refs[-1]
    for offset, ref in enumerate(refs[:-1]):
        out_ref[place_ref[1] ^ offset] = ref[...].astype(F32)


def gather(place, parts):
    own, samples = parts[0].shape
    return pl.pallas_call(
        gather_kernel,
        out_shape=jax.ShapeDtypeStruct((len(parts), own, samples), F32),
        in_specs=[SMEM] + [VMEM] * len(parts),
        out_specs=VMEM,
        compiler_params=params(16),
    )(place, *parts)


def per_device(templates, channel_mask, waveforms, waveform_tail):
    length = templates.shape[-1]
    samples = waveforms.shape[-1]
    halo = waveform_tail.shape[-1]
    tm_count = lax.axis_size("tm")
    chips = lax.axis_size("sta") // 2
    tm_index, sta_index = lax.axis_index("tm"), lax.axis_index("sta")
    place = jnp.stack([sta_index // 2, tm_index, sta_index % 2]).astype(jnp.int32)
    tpl = jnp.transpose(templates[0, :, 0], (1, 2, 0))
    mask = channel_mask[..., 0]
    rows = tpl.shape[-1] // chips
    packed = pack(place, tpl, mask, waveforms[0], waveform_tail[0], chips)
    messages, wave = packed[:chips], packed[chips]
    waves = [wave] + [swap_with(wave, "sta", 2 * offset) for offset in range(1, chips)]
    pieces = [messages[0]] + [swap_with(messages[offset], "sta", 2 * offset) for offset in range(1, chips)]
    stacked = jnp.stack([part[:, :samples] for part in waves])
    shards = [stacked] + [swap_with(stacked, "tm", offset) for offset in range(1, tm_count)]
    ext, inv = wave_windows(place, shards, waves, length, halo)
    acc = None
    for offset in range(chips):
        acc = piece(offset, rows, length, pieces[offset], ext, inv, acc)
    keep, send = split(place, acc)
    parts = shard(place, keep, swap_with(send, "sta", 1), tm_count)
    parts = [parts[0]] + [swap_with(parts[offset], "tm", offset) for offset in range(1, tm_count)]
    return gather(place, parts)


def solution(mesh):
    placed = (
        P("tm", None, "sta", None, None),
        P("tm", None, "sta"),
        P("sta", None, "tm"),
        P("sta", None, None),
    )
    return jax.shard_map(
        per_device, mesh=mesh, in_specs=placed, out_specs=P(None, "sta", "tm"), check_vma=False
    )
```

```python
import functools
import jax
import jax.numpy as jnp
from jax import lax
from jax.experimental import pallas as pl
from jax.experimental.pallas import tpu as pltpu
from jax.sharding import PartitionSpec as P

F32 = jnp.float32
BF16 = jnp.bfloat16
LANES = 128
CHUNK = 512
VMEM = pl.BlockSpec(memory_space=pltpu.VMEM)
SMEM = pl.BlockSpec(memory_space=pltpu.SMEM)
HBM = pl.BlockSpec(memory_space=pltpu.HBM)
CHEAP = pl.CostEstimate(flops=1, bytes_accessed=1, transcendentals=0)


def params(limit_mib):
    return pltpu.CompilerParams(vmem_limit_bytes=limit_mib << 20)


def up(value, multiple):
    return (value + multiple - 1) // multiple * multiple


def swap_with(x, axis, offset):
    size = lax.axis_size(axis)
    return lax.ppermute(x, axis, [(i, i ^ offset) for i in range(size)])


def join_kernel(wave_ref, tail_ref, out_ref, wave_held, tail_held, arrived):
    copies = [
        pltpu.make_async_copy(wave_ref, wave_held, arrived.at[0]),
        pltpu.make_async_copy(tail_ref, tail_held, arrived.at[1]),
    ]
    for copy in copies:
        copy.start()
    for copy in copies:
        copy.wait()
    samples = wave_held.shape[-1]
    out_ref[...] = jnp.zeros_like(out_ref)
    out_ref[:, :samples] = wave_held[...]
    out_ref[:, samples : samples + tail_held.shape[-1]] = tail_held[...]


def join(wave, tail):
    return pl.pallas_call(
        join_kernel,
        out_shape=jax.ShapeDtypeStruct((wave.shape[0], up(wave.shape[-1] + tail.shape[-1], LANES)), BF16),
        in_specs=[HBM] * 2,
        out_specs=VMEM,
        scratch_shapes=[pltpu.VMEM(x.shape, x.dtype) for x in (wave, tail)] + [pltpu.SemaphoreType.DMA((2,))],
        compiler_params=params(16),
        cost_estimate=CHEAP,
    )(*[pltpu.with_memory_space_constraint(x, pltpu.HBM) for x in (wave, tail)])


def pack_kernel(chips, rows, length, place_ref, tpl_ref, mask_ref, *refs):
    tpl_outs, (held_ref, mask_held, arrived) = refs[:chips], refs[chips:]
    comps = tpl_ref.shape[0]
    copies = [pltpu.make_async_copy(mask_ref, mask_held, arrived.at[comps])]
    copies += [pltpu.make_async_copy(tpl_ref.at[c], held_ref.at[c], arrived.at[c]) for c in range(comps)]
    for copy in copies:
        copy.start()
    copies[0].wait()
    folds = LANES // rows
    fold_lags = tpl_outs[0].shape[1]
    lane = lax.broadcasted_iota(jnp.int32, (1, LANES), 1)
    for comp in range(comps):
        copies[1 + comp].wait()
        for offset in range(chips):
            target = place_ref[0] ^ offset
            tile = pl.multiple_of((target * rows) // LANES * LANES, LANES)
            start = (target * rows) % LANES
            mask = mask_held[:, pl.ds(tile, LANES)].astype(F32)
            values = held_ref[comp, :, pl.ds(tile, LANES)].astype(F32) * mask
            folded = jnp.zeros((fold_lags, LANES), F32)
            for fold in range(folds):
                piece = values[fold * fold_lags : min((fold + 1) * fold_lags, length)]
                if piece.shape[0] == 0:
                    continue
                if piece.shape[0] < fold_lags:
                    piece = jnp.concatenate(
                        [piece, jnp.zeros((fold_lags - piece.shape[0], LANES), F32)], axis=0
                    )
                turned = pltpu.roll(piece, (fold * rows - start + LANES) % LANES, 1)
                here = (lane >= fold * rows) & (lane < (fold + 1) * rows)
                folded = jnp.where(here, turned, folded)
            tpl_outs[offset][comp] = folded.astype(BF16)


def pack(place, tpl, mask, chips):
    comps, length, all_rows = tpl.shape
    rows = all_rows // chips
    fold_lags = up(-(-length // (LANES // rows)), 16)
    return pl.pallas_call(
        functools.partial(pack_kernel, chips, rows, length),
        out_shape=[jax.ShapeDtypeStruct((comps, fold_lags, LANES), BF16)] * chips,
        in_specs=[SMEM] + [HBM] * 2,
        out_specs=[VMEM] * chips,
        scratch_shapes=[pltpu.VMEM(x.shape, x.dtype) for x in (tpl, mask)]
        + [pltpu.SemaphoreType.DMA((comps + 1,))],
        compiler_params=params(16),
        cost_estimate=CHEAP,
    )(place, *[pltpu.with_memory_space_constraint(x, pltpu.HBM) for x in (tpl, mask)])


def wave_kernel(shards, chips, length, halo, place_ref, *refs):
    shard_refs, tail_refs = refs[:shards], refs[shards : shards + chips]
    ext_ref, inv_ref = refs[shards + chips :]
    comps, samples = shard_refs[0].shape[1:]
    total = inv_ref.shape[-1]
    width = ext_ref.shape[-1]
    ext_ref[...] = jnp.zeros_like(ext_ref)
    for chip in range(chips):
        for offset in range(shards):
            at = pl.multiple_of((place_ref[1] ^ offset) * samples, LANES)
            ext_ref[chip * comps : (chip + 1) * comps, pl.ds(at, samples)] = shard_refs[offset][chip].astype(F32)
        ext_ref[chip * comps : (chip + 1) * comps, total : total + halo] = tail_refs[chip][
            :, samples : samples + halo
        ].astype(F32)

    def window(values):
        result, done, span, doubled = None, 0, 1, values
        while span <= length:
            if length & span:
                part = doubled if done == 0 else pltpu.roll(doubled, width - done, 1)
                result = part if result is None else result + part
                done += span
            span *= 2
            if span <= length:
                doubled = doubled + pltpu.roll(doubled, width - span // 2, 1)
        return result[:, :total]

    values = ext_ref[...]
    window_sum = window(values)
    window_square = window(values * values)
    inv_ref[...] = lax.rsqrt(window_square - window_sum * window_sum / length + 1e-05)


def wave_windows(place, shards, tails, length, halo):
    chips, comps, samples = shards[0].shape
    total = samples * len(shards)
    width = total + up(length, LANES)
    return pl.pallas_call(
        functools.partial(wave_kernel, len(shards), chips, length, halo),
        out_shape=[
            jax.ShapeDtypeStruct((chips * comps, width), F32),
            jax.ShapeDtypeStruct((chips * comps, total), F32),
        ],
        in_specs=[SMEM] + [VMEM] * (len(shards) + chips),
        out_specs=[VMEM] * 2,
        compiler_params=params(16),
        cost_estimate=CHEAP,
    )(place, *shards, *tails)


def lag_rows(values, rows, length):
    fold_lags = values.shape[0]
    folds = LANES // rows
    splits = -(-length // (2 * LANES))

    def over_folds(total):
        span = rows
        while span < LANES:
            total = total + pltpu.roll(total, span, 1)
            span *= 2
        return total

    lane = lax.broadcasted_iota(jnp.int32, values.shape, 1)
    lag = lax.broadcasted_iota(jnp.int32, values.shape, 0) + lane // rows * fold_lags
    mean = over_folds(jnp.sum(values, axis=0, keepdims=True)) / length
    centred = jnp.where(lag < length, values - mean, 0.0)
    energy = over_folds(jnp.sum(centred * centred, axis=0, keepdims=True))
    weighted = centred * lax.rsqrt(energy + 1e-05)
    parts = [weighted] + [pltpu.roll(weighted, LANES - fold * rows, 1) for fold in range(1, folds)]
    wanted = splits * 2 * LANES
    if folds * fold_lags < wanted:
        parts.append(jnp.zeros((wanted - folds * fold_lags, LANES), F32))
    spread = jnp.concatenate(parts, axis=0)
    low = lax.broadcasted_iota(jnp.int32, (LANES, LANES), 1) < LANES // 2
    flip = (
        lax.broadcasted_iota(jnp.int32, (LANES, LANES), 0)
        + lax.broadcasted_iota(jnp.int32, (LANES, LANES), 1)
        == LANES - 1
    ).astype(BF16)
    result = []
    for split in range(splits):
        at = split * 2 * LANES
        both = jnp.where(low, spread[at : at + LANES], pltpu.roll(spread[at + LANES : at + 2 * LANES], LANES // 2, 1))
        turned = lax.dot_general(
            both.astype(BF16), flip, (((0,), (0,)), ((), ())), preferred_element_type=F32
        ).astype(BF16)
        result.append(jnp.concatenate([turned[:rows], turned[LANES // 2 : LANES // 2 + rows]], axis=1))
    return jnp.concatenate(result, axis=0)


def fill_hankel(row, out_ref):
    width = row.shape[-1]
    spread = jnp.broadcast_to(row.astype(BF16), (LANES, width))
    out_ref[...] = pltpu.roll(spread, width - (LANES - 1), 1, stride=1, stride_axis=0)


def hankel_kernel(index, ext_ref, out_ref):
    comps = out_ref.shape[0]
    for comp in range(comps):
        at = index * comps + comp
        fill_hankel(ext_ref[at : at + 1, :], out_ref.at[comp])


def hankel(index, comps, ext):
    return pl.pallas_call(
        functools.partial(hankel_kernel, index),
        out_shape=jax.ShapeDtypeStruct((comps, LANES, ext.shape[-1]), BF16),
        in_specs=[VMEM],
        out_specs=VMEM,
        compiler_params=params(16),
        cost_estimate=CHEAP,
    )(ext)


def piece_kernel(index, rows, length, last, place_ref, tpl_ref, ext_ref, inv_ref, *refs):
    refs = list(refs)
    acc_ref = None if index == 0 else refs.pop(0)
    given_ref = refs.pop(0) if last else None
    out_refs = [refs.pop(0) for _ in range(2 if last else 1)]
    hankel_ref, product_ref, sum_ref = refs
    sum_ref = sum_ref if last else out_refs[0]
    comps = tpl_ref.shape[0]
    total = inv_ref.shape[-1]
    reach = product_ref.shape[-1]
    splits = product_ref.shape[1] // rows
    if last:
        hankel_ref = given_ref
    else:
        for comp in range(comps):
            at = index * comps + comp
            fill_hankel(ext_ref[at : at + 1, :], hankel_ref.at[comp])
    lhs = [lag_rows(tpl_ref[comp].astype(F32), rows, length) for comp in range(comps)]
    for comp in range(comps):
        rhs = jnp.concatenate(
            [hankel_ref[comp, :, :reach], hankel_ref[comp, :, LANES : LANES + reach]], axis=0
        )
        product_ref[comp] = jnp.dot(lhs[comp], rhs, preferred_element_type=F32)
    for start in range(0, total, CHUNK):
        stop = min(start + CHUNK, total)
        chunk = None if acc_ref is None else acc_ref[:, start:stop]
        for comp in range(comps):
            at = index * comps + comp
            part = product_ref[comp, :rows, start:stop]
            for split in range(1, splits):
                shift = split * 2 * LANES
                part = part + product_ref[comp, split * rows : (split + 1) * rows, shift + start : shift + stop]
            part = part * inv_ref[at : at + 1, start:stop]
            chunk = part if chunk is None else chunk + part
        sum_ref[:, start:stop] = chunk
    if last:
        keep_ref, send_ref = out_refs
        own = rows // 2
        at = pl.multiple_of(place_ref[2] * own, own)
        other = pl.multiple_of((1 - place_ref[2]) * own, own)
        keep_ref[...] = sum_ref[pl.ds(at, own), :]
        send_ref[...] = sum_ref[pl.ds(other, own), :].astype(BF16)


def piece(place, index, rows, length, last, tpl, ext, inv, acc, given):
    total, width = inv.shape[-1], ext.shape[-1]
    comps = tpl.shape[0]
    splits = -(-length // (2 * LANES))
    reach = total + (splits - 1) * 2 * LANES
    inputs = [place, tpl, ext, inv] + [part for part in (acc, given) if part is not None]
    out_shape = [jax.ShapeDtypeStruct((rows, total), F32)]
    if last:
        half = (rows // 2, total)
        out_shape = [jax.ShapeDtypeStruct(half, F32), jax.ShapeDtypeStruct(half, BF16)]
    return pl.pallas_call(
        functools.partial(piece_kernel, index, rows, length, last),
        out_shape=out_shape,
        in_specs=[SMEM] + [VMEM] * (len(inputs) - 1),
        out_specs=[VMEM] * len(out_shape),
        scratch_shapes=[
            pltpu.VMEM((1, LANES, LANES) if last else (comps, LANES, width), BF16),
            pltpu.VMEM((comps, splits * rows, reach), F32),
            pltpu.VMEM((rows, total) if last else (8, LANES), F32),
        ],
        compiler_params=params(24),
        cost_estimate=CHEAP,
    )(*inputs)


def shard_kernel(place_ref, keep_ref, came_ref, own_ref, *send_refs):
    samples = own_ref.shape[-1]
    for offset, ref in enumerate((own_ref,) + send_refs):
        at = pl.multiple_of((place_ref[1] ^ offset) * samples, LANES)
        total = keep_ref[:, pl.ds(at, samples)] + came_ref[:, pl.ds(at, samples)].astype(F32)
        ref[...] = total.astype(ref.dtype)


def shard(place, keep, came, count):
    own, total = keep.shape
    samples = total // count
    return pl.pallas_call(
        shard_kernel,
        out_shape=[jax.ShapeDtypeStruct((own, samples), F32)]
        + [jax.ShapeDtypeStruct((own, samples), BF16)] * (count - 1),
        in_specs=[SMEM, VMEM, VMEM],
        out_specs=[VMEM] * count,
        compiler_params=params(16),
        cost_estimate=CHEAP,
    )(place, keep, came)


def gather_kernel(place_ref, *refs):
    out_ref = refs[-1]
    for offset, ref in enumerate(refs[:-1]):
        out_ref[place_ref[1] ^ offset] = ref[...].astype(F32)


def gather(place, parts):
    own, samples = parts[0].shape
    return pl.pallas_call(
        gather_kernel,
        out_shape=jax.ShapeDtypeStruct((len(parts), own, samples), F32),
        in_specs=[SMEM] + [VMEM] * len(parts),
        out_specs=VMEM,
        compiler_params=params(16),
    )(place, *parts)


def per_device(templates, channel_mask, waveforms, waveform_tail):
    length = templates.shape[-1]
    samples = waveforms.shape[-1]
    halo = waveform_tail.shape[-1]
    tm_count = lax.axis_size("tm")
    chips = lax.axis_size("sta") // 2
    tm_index, sta_index = lax.axis_index("tm"), lax.axis_index("sta")
    place = jnp.stack([sta_index // 2, tm_index, sta_index % 2]).astype(jnp.int32)
    tpl = jnp.transpose(templates[0, :, 0], (1, 2, 0))
    mask = channel_mask[..., 0]
    rows = tpl.shape[-1] // chips
    wave = join(waveforms[0], waveform_tail[0])
    waves = [wave] + [swap_with(wave, "sta", 2 * offset) for offset in range(1, chips)]
    messages = pack(place, tpl, mask, chips)
    messages, waves = lax.optimization_barrier((messages, waves))
    pieces = {offset: swap_with(messages[offset], "sta", 2 * offset) for offset in range(2, chips)}
    stacked = jnp.stack([part[:, :samples] for part in waves])
    shards = [stacked] + [swap_with(stacked, "tm", offset) for offset in range(1, tm_count)]
    near, shards = lax.optimization_barrier((messages[1], shards))
    pieces[0], pieces[1] = messages[0], swap_with(near, "sta", 2)
    ext, inv = wave_windows(place, shards, waves, length, halo)
    acc = None
    order = [0] + list(range(chips - 1, 2, -1)) + [1, 2]
    given = hankel(order[-1], waveforms.shape[1], ext)
    for offset in order:
        last = offset == order[-1]
        *done, acc = piece(
            place, offset, rows, length, last, pieces[offset], ext, inv, acc, given if last else None
        )
    keep, send = done[0], acc
    parts = shard(place, keep, swap_with(send, "sta", 1), tm_count)
    parts = [parts[0]] + [swap_with(parts[offset], "tm", offset) for offset in range(1, tm_count)]
    return gather(place, parts)


def solution(mesh):
    placed = (
        P("tm", None, "sta", None, None),
        P("tm", None, "sta"),
        P("sta", None, "tm"),
        P("sta", None, None),
    )
    return jax.shard_map(
        per_device, mesh=mesh, in_specs=placed, out_specs=P(None, "sta", "tm"), check_vma=False
    )
```

```python
import functools
import jax
import jax.numpy as jnp
from jax import lax
from jax.experimental import pallas as pl
from jax.experimental.pallas import tpu as pltpu
from jax.sharding import PartitionSpec as P

F32 = jnp.float32
BF16 = jnp.bfloat16
LANES = 128
CHUNK = 512
EXTRA = 8
VMEM = pl.BlockSpec(memory_space=pltpu.VMEM)
SMEM = pl.BlockSpec(memory_space=pltpu.SMEM)
HBM = pl.BlockSpec(memory_space=pltpu.HBM)
COSTS = (500000000, 1, 500000000)
CHEAP = pl.CostEstimate(flops=1, bytes_accessed=1, transcendentals=0)


def params(limit_mib):
    return pltpu.CompilerParams(vmem_limit_bytes=limit_mib << 20)


def up(value, multiple):
    return (value + multiple - 1) // multiple * multiple


def swap_with(x, axis, offset):
    size = lax.axis_size(axis)
    return lax.ppermute(x, axis, [(i, i ^ offset) for i in range(size)])


def join_kernel(wave_ref, tail_ref, out_ref, wave_held, tail_held, arrived):
    copies = [
        pltpu.make_async_copy(wave_ref, wave_held, arrived.at[0]),
        pltpu.make_async_copy(tail_ref, tail_held, arrived.at[1]),
    ]
    for copy in copies:
        copy.start()
    for copy in copies:
        copy.wait()
    samples = wave_held.shape[-1]
    out_ref[...] = jnp.zeros_like(out_ref)
    out_ref[:, :samples] = wave_held[...]
    out_ref[:, samples : samples + tail_held.shape[-1]] = tail_held[...]


def join(wave, tail):
    return pl.pallas_call(
        join_kernel,
        out_shape=jax.ShapeDtypeStruct((wave.shape[0], up(wave.shape[-1] + tail.shape[-1], LANES)), BF16),
        in_specs=[HBM] * 2,
        out_specs=VMEM,
        scratch_shapes=[pltpu.VMEM(x.shape, x.dtype) for x in (wave, tail)] + [pltpu.SemaphoreType.DMA((2,))],
        compiler_params=params(16),
        cost_estimate=CHEAP,
    )(*[pltpu.with_memory_space_constraint(x, pltpu.HBM) for x in (wave, tail)])


def fold_lags(rows, length):
    return up(-(-length // (LANES // rows)), 8)


def pack_kernel(parts, rows, length, starts_ref, tpl_ref, mask_ref, *refs):
    tpl_outs, (held_ref, mask_held, arrived) = refs[: len(parts)], refs[len(parts) :]
    lags = fold_lags(rows, length)
    comps = tpl_ref.shape[0]
    copies = [pltpu.make_async_copy(mask_ref, mask_held, arrived.at[comps])]
    copies += [pltpu.make_async_copy(tpl_ref.at[c], held_ref.at[c], arrived.at[c]) for c in range(comps)]
    for copy in copies:
        copy.start()
    copies[0].wait()
    lane = lax.broadcasted_iota(jnp.int32, (1, LANES), 1)
    for comp in range(comps):
        copies[1 + comp].wait()
        for index, (low, high) in enumerate(parts):
            if not low <= comp < high:
                continue
            row = starts_ref[index]
            tile = pl.multiple_of(row // LANES * LANES, LANES)
            mask = mask_held[:, pl.ds(tile, LANES)].astype(F32)
            values = held_ref[comp, :, pl.ds(tile, LANES)].astype(F32) * mask
            folded = jnp.zeros((lags, LANES), F32)
            for fold in range(LANES // rows):
                piece = values[fold * lags : min((fold + 1) * lags, length)]
                if piece.shape[0] == 0:
                    continue
                if piece.shape[0] < lags:
                    piece = jnp.concatenate([piece, jnp.zeros((lags - piece.shape[0], LANES), F32)], axis=0)
                turned = pltpu.roll(piece, (fold * rows - row % LANES + LANES) % LANES, 1)
                here = (lane >= fold * rows) & (lane < (fold + 1) * rows)
                folded = jnp.where(here, turned, folded)
            tpl_outs[index][comp - low] = folded.astype(BF16)


def pack(starts, parts, rows, tpl, mask):
    comps, length, _ = tpl.shape
    lags = fold_lags(rows, length)
    return pl.pallas_call(
        functools.partial(pack_kernel, parts, rows, length),
        out_shape=[jax.ShapeDtypeStruct((high - low, lags, LANES), BF16) for low, high in parts],
        in_specs=[SMEM] + [HBM] * 2,
        out_specs=[VMEM] * len(parts),
        scratch_shapes=[pltpu.VMEM(x.shape, x.dtype) for x in (tpl, mask)]
        + [pltpu.SemaphoreType.DMA((comps + 1,))],
        compiler_params=params(16),
        cost_estimate=CHEAP,
    )(starts, *[pltpu.with_memory_space_constraint(x, pltpu.HBM) for x in (tpl, mask)])


def fill_samples(halo, tm_index, shard_refs, tail_refs, ext_ref):
    chips, comps, samples = shard_refs[0].shape
    total = samples * len(shard_refs)
    ext_ref[...] = jnp.zeros_like(ext_ref)
    for chip in range(chips):
        at = chip * comps
        for offset, ref in enumerate(shard_refs):
            start = pl.multiple_of((tm_index ^ offset) * samples, LANES)
            ext_ref[at : at + comps, pl.ds(start, samples)] = ref[chip].astype(F32)
        ext_ref[at : at + comps, total : total + halo] = tail_refs[chip][:, samples : samples + halo].astype(F32)


def fill_inverse(length, ext_ref, both_ref, inv_ref):
    count, width = ext_ref.shape
    total = inv_ref.shape[-1]
    both_ref[:count, :] = ext_ref[...]
    both_ref[count : 2 * count, :] = ext_ref[...] * ext_ref[...]
    result, done, span, doubled = None, 0, 1, both_ref[: 2 * count, :]
    while span <= length:
        if length & span:
            part = doubled if done == 0 else pltpu.roll(doubled, width - done, 1)
            result = part if result is None else result + part
            done += span
        span *= 2
        if span <= length:
            doubled = doubled + pltpu.roll(doubled, width - span // 2, 1)
    both_ref[: 2 * count, :] = result
    window_sum = both_ref[:count, :total]
    window_square = both_ref[count : 2 * count, :total]
    inv_ref[...] = lax.rsqrt(window_square - window_sum * window_sum / length + 1e-05)


def lag_rows(values, rows, length):
    lags = values.shape[0]
    folds = LANES // rows
    splits = -(-length // (2 * LANES))

    def over_folds(total):
        span = rows
        while span < LANES:
            total = total + pltpu.roll(total, span, 1)
            span *= 2
        return total

    lane = lax.broadcasted_iota(jnp.int32, values.shape, 1)
    lag = lax.broadcasted_iota(jnp.int32, values.shape, 0) + lane // rows * lags
    mean = over_folds(jnp.sum(values, axis=0, keepdims=True)) / length
    centred = jnp.where(lag < length, values - mean, 0.0)
    energy = over_folds(jnp.sum(centred * centred, axis=0, keepdims=True))
    weighted = centred * lax.rsqrt(energy + 1e-05)
    parts = [weighted] + [pltpu.roll(weighted, LANES - fold * rows, 1) for fold in range(1, folds)]
    wanted = splits * 2 * LANES
    if folds * lags < wanted:
        parts.append(jnp.zeros((wanted - folds * lags, LANES), F32))
    spread = jnp.concatenate(parts, axis=0)
    low = lax.broadcasted_iota(jnp.int32, (LANES, LANES), 1) < LANES // 2
    flip = (
        lax.broadcasted_iota(jnp.int32, (LANES, LANES), 0)
        + lax.broadcasted_iota(jnp.int32, (LANES, LANES), 1)
        == LANES - 1
    ).astype(BF16)
    result = []
    for split in range(splits):
        at = split * 2 * LANES
        both = jnp.where(low, spread[at : at + LANES], pltpu.roll(spread[at + LANES : at + 2 * LANES], LANES // 2, 1))
        turned = lax.dot_general(
            both.astype(BF16), flip, (((0,), (0,)), ((), ())), preferred_element_type=F32
        )
        result.append(jnp.concatenate([turned[:rows], turned[LANES // 2 : LANES // 2 + rows]], axis=1))
    return jnp.concatenate(result, axis=0).astype(BF16)


def fill_hankel(row, out_ref):
    width = row.shape[-1]
    spread = jnp.broadcast_to(row.astype(BF16), (LANES, width))
    out_ref[...] = pltpu.roll(spread, width - (LANES - 1), 1, stride=1, stride_axis=0)


def multiply(ext_at, rows, length, tpl_ref, ext_ref, work_refs):
    hankel_ref, product_ref = work_refs
    reach = product_ref.shape[-1]
    for comp in range(tpl_ref.shape[0]):
        fill_hankel(ext_ref[ext_at + comp : ext_at + comp + 1, :], hankel_ref.at[comp])
    lhs = [lag_rows(tpl_ref[comp].astype(F32), rows, length) for comp in range(tpl_ref.shape[0])]
    for comp in range(tpl_ref.shape[0]):
        rhs = jnp.concatenate(
            [hankel_ref[comp, :, :reach], hankel_ref[comp, :, LANES : LANES + reach]], axis=0
        )
        product_ref[comp] = jnp.dot(lhs[comp], rhs, preferred_element_type=F32)


def collect(inv_at, rows, comps, inv_ref, acc_refs, work_refs, store):
    product_ref = work_refs[1]
    splits = product_ref.shape[1] // rows
    total = product_ref.shape[-1] - (splits - 1) * 2 * LANES
    for start in range(0, total, CHUNK):
        stop = min(start + CHUNK, total)
        chunk = None
        for ref in acc_refs:
            part = ref[:, start:stop]
            chunk = part if chunk is None else chunk + part
        for comp in range(comps):
            part = product_ref[comp, :rows, start:stop]
            for split in range(1, splits):
                shift = split * 2 * LANES
                part = part + product_ref[comp, split * rows : (split + 1) * rows, shift + start : shift + stop]
            part = part * inv_ref[inv_at + comp : inv_at + comp + 1, start:stop]
            chunk = part if chunk is None else chunk + part
        store(start, stop, chunk)


def correlate(at, rows, length, tpl_ref, ext_ref, inv_ref, acc_refs, work_refs, store):
    multiply(at, rows, length, tpl_ref, ext_ref, work_refs)
    collect(at, rows, tpl_ref.shape[0], inv_ref, acc_refs, work_refs, store)


def storing(ref):
    def store(start, stop, chunk):
        ref[:, start:stop] = chunk

    return store


def first_kernel(shards, chips, rows, length, halo, place_ref, tpl_ref, *refs):
    shard_refs, tail_refs = refs[:shards], refs[shards : shards + chips]
    ext_ref, inv_ref, sum_ref, both_ref, *work_refs = refs[shards + chips :]
    fill_samples(halo, place_ref[1], shard_refs, tail_refs, ext_ref)
    multiply(0, rows, length, tpl_ref, ext_ref, work_refs)
    fill_inverse(length, ext_ref, both_ref, inv_ref)
    collect(0, rows, tpl_ref.shape[0], inv_ref, [], work_refs, storing(sum_ref))


def middle_kernel(at, rows, length, tpl_ref, ext_ref, inv_ref, acc_ref, sum_ref, *work_refs):
    correlate(at, rows, length, tpl_ref, ext_ref, inv_ref, [acc_ref], work_refs, storing(sum_ref))


def parting_kernel(at, rows, length, place_ref, tpl_ref, ext_ref, inv_ref, acc_ref, keep_ref, send_ref, *work_refs):
    own = rows // 2
    low = place_ref[2] == 0

    def store(start, stop, chunk):
        keep_ref[:, start:stop] = jnp.where(low, chunk[:own], chunk[own:])
        send_ref[:, start:stop] = jnp.where(low, chunk[own:], chunk[:own]).astype(BF16)

    correlate(at, rows, length, tpl_ref, ext_ref, inv_ref, [acc_ref], work_refs, store)


def work_buffers(comps, rows, total, width, length):
    splits = -(-length // (2 * LANES))
    reach = total + (splits - 1) * 2 * LANES
    return [pltpu.VMEM((comps, LANES, width), BF16), pltpu.VMEM((comps, splits * rows, reach), F32)]


def first(place, rows, length, halo, tpl, shards, tails):
    chips, comps, samples = shards[0].shape
    total = samples * len(shards)
    width = total + up(length, LANES)
    count = chips * comps
    return pl.pallas_call(
        functools.partial(first_kernel, len(shards), chips, rows, length, halo),
        out_shape=[
            jax.ShapeDtypeStruct((count, width), F32),
            jax.ShapeDtypeStruct((count, total), F32),
            jax.ShapeDtypeStruct((rows, total), F32),
        ],
        in_specs=[SMEM] + [VMEM] * (1 + len(shards) + chips),
        out_specs=[VMEM] * 3,
        scratch_shapes=[pltpu.VMEM((up(2 * count, 8), width), F32)]
        + work_buffers(comps, rows, total, width, length),
        compiler_params=params(24),
        cost_estimate=CHEAP,
    )(place, tpl, *shards, *tails)


def later(kernel, place, rows, total, length, out_shape, inputs, scratch=(), flops=1):
    comps, width = inputs[0].shape[0], inputs[1].shape[-1]
    given = ([] if place is None else [place]) + list(inputs)
    specs = [VMEM] * len(inputs) if place is None else [SMEM] + [VMEM] * len(inputs)
    return pl.pallas_call(
        kernel,
        out_shape=out_shape,
        in_specs=specs,
        out_specs=[VMEM] * len(out_shape),
        scratch_shapes=list(scratch) + work_buffers(comps, rows, total, width, length),
        compiler_params=params(24),
        cost_estimate=pl.CostEstimate(flops=flops, bytes_accessed=1, transcendentals=0),
    )(*given)


def shard_kernel(place_ref, keep_ref, came_ref, own_ref, *send_refs):
    samples = own_ref.shape[-1]
    for offset, ref in enumerate((own_ref,) + send_refs):
        at = pl.multiple_of((place_ref[1] ^ offset) * samples, LANES)
        total = keep_ref[:, pl.ds(at, samples)] + came_ref[:, pl.ds(at, samples)].astype(F32)
        total = total.astype(ref.dtype)
        if ref.shape[0] > total.shape[0]:
            total = jnp.concatenate([total, jnp.zeros((ref.shape[0] - total.shape[0], samples), ref.dtype)], axis=0)
        ref[...] = total


def shard(place, keep, came, count):
    own, total = keep.shape
    samples = total // count
    return pl.pallas_call(
        shard_kernel,
        out_shape=[jax.ShapeDtypeStruct((own, samples), F32)]
        + [
            jax.ShapeDtypeStruct((own + (EXTRA if offset & (offset - 1) else 0), samples), BF16)
            for offset in range(1, count)
        ],
        in_specs=[SMEM, VMEM, VMEM],
        out_specs=[VMEM] * count,
        compiler_params=params(16),
        cost_estimate=CHEAP,
    )(place, keep, came)


def gather_kernel(place_ref, *refs):
    *part_refs, out_ref, held_ref, left = refs
    copies = []
    for offset, ref in enumerate(part_refs):
        held_ref[offset] = ref[: out_ref.shape[1], :].astype(F32)
        copies.append(
            pltpu.make_async_copy(held_ref.at[offset], out_ref.at[place_ref[1] ^ offset], left.at[offset])
        )
        copies[-1].start()
    for copy in copies:
        copy.wait()


def gather(place, parts):
    shape = (len(parts),) + parts[0].shape
    return pl.pallas_call(
        gather_kernel,
        out_shape=jax.ShapeDtypeStruct(shape, F32),
        in_specs=[SMEM] + [VMEM] * len(parts),
        out_specs=HBM,
        scratch_shapes=[pltpu.VMEM(shape, F32), pltpu.SemaphoreType.DMA((len(parts),))],
        compiler_params=params(16),
    )(place, *parts)


def per_device(templates, channel_mask, waveforms, waveform_tail):
    length = templates.shape[-1]
    samples = waveforms.shape[-1]
    halo = waveform_tail.shape[-1]
    tm_count = lax.axis_size("tm")
    chips = lax.axis_size("sta") // 2
    tm_index, sta_index = lax.axis_index("tm"), lax.axis_index("sta")
    chip_index, core_index = sta_index // 2, sta_index % 2
    place = jnp.stack([chip_index, tm_index, core_index]).astype(jnp.int32)
    tpl = jnp.transpose(templates[0, :, 0], (1, 2, 0))
    mask = channel_mask[..., 0]
    rows = tpl.shape[-1] // chips
    own = rows // 2
    total = samples * tm_count
    comps = tpl.shape[0]
    final = chips // 2
    between = [1] + [offset for offset in range(chips - 1, 1, -1) if offset != final]

    wave = join(waveforms[0], waveform_tail[0])
    waves = [wave] + [swap_with(wave, "sta", 2 * offset) for offset in range(1, chips)]
    offsets = [0] + between + [final, final]
    parts = [(0, comps)] * (len(offsets) - 2) + [(0, comps - 1), (comps - 1, comps)]
    starts = jnp.stack([(chip_index ^ offset) * rows for offset in offsets]).astype(jnp.int32)
    messages = pack(starts, parts, rows, tpl, mask)
    messages, waves = lax.optimization_barrier((messages, waves))
    pieces = {offset: swap_with(messages[1 + i], "sta", 2 * offset) for i, offset in enumerate(between)}
    stacked = jnp.stack([part[:, :samples] for part in waves])
    shards = [stacked] + [swap_with(stacked, "tm", offset) for offset in range(1, tm_count)]
    late, shards = lax.optimization_barrier((messages[-2:], shards))
    late = [swap_with(part, "sta", 2 * final) for part in late]
    ext, inv, acc = first(place, rows, length, halo, messages[0], shards, waves)
    whole = jax.ShapeDtypeStruct((rows, total), F32)
    stations = [(offset * comps, pieces[offset]) for offset in between] + [(final * comps, late[0])]
    for step, (at, piece) in enumerate(stations):
        kernel = functools.partial(middle_kernel, at, rows, length)
        flops = COSTS[min(step, len(COSTS) - 1)]
        (acc,) = later(kernel, None, rows, total, length, [whole], [piece, ext, inv, acc], flops=flops)
    kernel = functools.partial(parting_kernel, final * comps + comps - 1, rows, length)
    halves = [jax.ShapeDtypeStruct((own, total), F32), jax.ShapeDtypeStruct((own, total), BF16)]
    keep, send = later(kernel, place, rows, total, length, halves, [late[1], ext, inv, acc])
    parts = shard(place, keep, swap_with(send, "sta", 1), tm_count)
    parts = [parts[0]] + [swap_with(parts[offset], "tm", offset) for offset in range(1, tm_count)]
    return gather(place, parts)


def solution(mesh):
    placed = (
        P("tm", None, "sta", None, None),
        P("tm", None, "sta"),
        P("sta", None, "tm"),
        P("sta", None, None),
    )
    return jax.shard_map(
        per_device, mesh=mesh, in_specs=placed, out_specs=P(None, "sta", "tm"), check_vma=False
    )
```

```python
import functools
import jax
import jax.numpy as jnp
from jax import lax
from jax.experimental import pallas as pl
from jax.experimental.pallas import tpu as pltpu
from jax.sharding import PartitionSpec as P

F32 = jnp.float32
BF16 = jnp.bfloat16
LANES = 128
CHUNK = 512
EXTRA = 8
VMEM = pl.BlockSpec(memory_space=pltpu.VMEM)
HBM = pl.BlockSpec(memory_space=pltpu.HBM)
F_MID, F_PART, F_JOIN, F_CLOSE = 500000000, 1, 500000000, 1
CHEAP = pl.CostEstimate(flops=1, bytes_accessed=1, transcendentals=0)


def params(limit_mib):
    return pltpu.CompilerParams(vmem_limit_bytes=limit_mib << 20)


def up(value, multiple):
    return (value + multiple - 1) // multiple * multiple


def swap_with(x, axis, offset):
    size = lax.axis_size(axis)
    return lax.ppermute(x, axis, [(i, i ^ offset) for i in range(size)])


def join_kernel(wave_ref, tail_ref, out_ref, wave_held, tail_held, arrived):
    copies = [
        pltpu.make_async_copy(wave_ref, wave_held, arrived.at[0]),
        pltpu.make_async_copy(tail_ref, tail_held, arrived.at[1]),
    ]
    for copy in copies:
        copy.start()
    for copy in copies:
        copy.wait()
    samples = wave_held.shape[-1]
    out_ref[...] = jnp.zeros_like(out_ref)
    out_ref[:, :samples] = wave_held[...]
    out_ref[:, samples : samples + tail_held.shape[-1]] = tail_held[...]


def join(wave, tail):
    return pl.pallas_call(
        join_kernel,
        out_shape=jax.ShapeDtypeStruct((wave.shape[0], up(wave.shape[-1] + tail.shape[-1], LANES)), BF16),
        in_specs=[HBM] * 2,
        out_specs=VMEM,
        scratch_shapes=[pltpu.VMEM(x.shape, x.dtype) for x in (wave, tail)] + [pltpu.SemaphoreType.DMA((2,))],
        compiler_params=params(16),
        cost_estimate=CHEAP,
    )(*[pltpu.with_memory_space_constraint(x, pltpu.HBM) for x in (wave, tail)])


def first_row(chip_offset, core_offset, all_rows):
    index = lax.axis_index("sta")
    rows = all_rows // (lax.axis_size("sta") // 2)
    row = (index // 2 ^ chip_offset) * rows
    return row if core_offset is None else row + (index % 2 ^ core_offset) * (rows // 2)


def fold_lags(rows, length):
    return up(-(-length // (LANES // rows)), 8)


def pack_kernel(targets, counts, length, tpl_ref, mask_ref, *refs):
    tpl_outs, (held_ref, mask_held, arrived) = refs[: len(counts)], refs[len(counts) :]
    comps = tpl_ref.shape[0]
    copies = [pltpu.make_async_copy(mask_ref, mask_held, arrived.at[comps])]
    copies += [pltpu.make_async_copy(tpl_ref.at[c], held_ref.at[c], arrived.at[c]) for c in range(comps)]
    for copy in copies:
        copy.start()
    copies[0].wait()
    lane = lax.broadcasted_iota(jnp.int32, (1, LANES), 1)
    for comp in range(comps):
        copies[1 + comp].wait()
        for index, rows in enumerate(counts):
            lags = fold_lags(rows, length)
            row = first_row(*targets[index], tpl_ref.shape[-1])
            tile = pl.multiple_of(row // LANES * LANES, LANES)
            mask = mask_held[:, pl.ds(tile, LANES)].astype(F32)
            values = held_ref[comp, :, pl.ds(tile, LANES)].astype(F32) * mask
            folded = jnp.zeros((lags, LANES), F32)
            for fold in range(LANES // rows):
                piece = values[fold * lags : min((fold + 1) * lags, length)]
                if piece.shape[0] == 0:
                    continue
                if piece.shape[0] < lags:
                    piece = jnp.concatenate([piece, jnp.zeros((lags - piece.shape[0], LANES), F32)], axis=0)
                turned = pltpu.roll(piece, (fold * rows - row % LANES + LANES) % LANES, 1)
                here = (lane >= fold * rows) & (lane < (fold + 1) * rows)
                folded = jnp.where(here, turned, folded)
            tpl_outs[index][comp] = folded.astype(BF16)


def pack(targets, counts, tpl, mask):
    comps, length, _ = tpl.shape
    return pl.pallas_call(
        functools.partial(pack_kernel, targets, counts, length),
        out_shape=[jax.ShapeDtypeStruct((comps, fold_lags(rows, length), LANES), BF16) for rows in counts],
        in_specs=[HBM] * 2,
        out_specs=[VMEM] * len(counts),
        scratch_shapes=[pltpu.VMEM(x.shape, x.dtype) for x in (tpl, mask)]
        + [pltpu.SemaphoreType.DMA((comps + 1,))],
        compiler_params=params(16),
        cost_estimate=CHEAP,
    )(*[pltpu.with_memory_space_constraint(x, pltpu.HBM) for x in (tpl, mask)])


def fill_samples(halo, tm_index, shard_refs, tail_refs, ext_ref):
    chips, comps, samples = shard_refs[0].shape
    total = samples * len(shard_refs)
    ext_ref[...] = jnp.zeros_like(ext_ref)
    for chip in range(chips):
        at = chip * comps
        for offset, ref in enumerate(shard_refs):
            start = pl.multiple_of((tm_index ^ offset) * samples, LANES)
            ext_ref[at : at + comps, pl.ds(start, samples)] = ref[chip].astype(F32)
        ext_ref[at : at + comps, total : total + halo] = tail_refs[chip][:, samples : samples + halo].astype(F32)


def fill_inverse(length, ext_ref, both_ref, inv_ref):
    count, width = ext_ref.shape
    total = inv_ref.shape[-1]
    both_ref[:count, :] = ext_ref[...]
    both_ref[count : 2 * count, :] = ext_ref[...] * ext_ref[...]
    result, done, span, doubled = None, 0, 1, both_ref[: 2 * count, :]
    while span <= length:
        if length & span:
            part = doubled if done == 0 else pltpu.roll(doubled, width - done, 1)
            result = part if result is None else result + part
            done += span
        span *= 2
        if span <= length:
            doubled = doubled + pltpu.roll(doubled, width - span // 2, 1)
    both_ref[: 2 * count, :] = result
    window_sum = both_ref[:count, :total]
    window_square = both_ref[count : 2 * count, :total]
    inv_ref[...] = lax.rsqrt(window_square - window_sum * window_sum / length + 1e-05)


def lag_rows(values, rows, length):
    lags = values.shape[0]
    folds = LANES // rows
    splits = -(-length // (2 * LANES))

    def over_folds(total):
        span = rows
        while span < LANES:
            total = total + pltpu.roll(total, span, 1)
            span *= 2
        return total

    lane = lax.broadcasted_iota(jnp.int32, values.shape, 1)
    lag = lax.broadcasted_iota(jnp.int32, values.shape, 0) + lane // rows * lags
    mean = over_folds(jnp.sum(values, axis=0, keepdims=True)) / length
    centred = jnp.where(lag < length, values - mean, 0.0)
    energy = over_folds(jnp.sum(centred * centred, axis=0, keepdims=True))
    weighted = centred * lax.rsqrt(energy + 1e-05)
    parts = [weighted] + [pltpu.roll(weighted, LANES - fold * rows, 1) for fold in range(1, folds)]
    wanted = splits * 2 * LANES
    if folds * lags < wanted:
        parts.append(jnp.zeros((wanted - folds * lags, LANES), F32))
    spread = jnp.concatenate(parts, axis=0)
    low = lax.broadcasted_iota(jnp.int32, (LANES, LANES), 1) < LANES // 2
    flip = (
        lax.broadcasted_iota(jnp.int32, (LANES, LANES), 0)
        + lax.broadcasted_iota(jnp.int32, (LANES, LANES), 1)
        == LANES - 1
    ).astype(BF16)
    result = []
    for split in range(splits):
        at = split * 2 * LANES
        both = jnp.where(low, spread[at : at + LANES], pltpu.roll(spread[at + LANES : at + 2 * LANES], LANES // 2, 1))
        turned = lax.dot_general(
            both.astype(BF16), flip, (((0,), (0,)), ((), ())), preferred_element_type=F32
        )
        result.append(jnp.concatenate([turned[:rows], turned[LANES // 2 : LANES // 2 + rows]], axis=1))
    return jnp.concatenate(result, axis=0).astype(BF16)


def fill_hankel(row, out_ref):
    width = row.shape[-1]
    spread = jnp.broadcast_to(row.astype(BF16), (LANES, width))
    out_ref[...] = pltpu.roll(spread, width - (LANES - 1), 1, stride=1, stride_axis=0)


def multiply(ext_at, rows, length, tpl_ref, ext_ref, work_refs):
    hankel_ref, product_ref = work_refs
    reach = product_ref.shape[-1]
    for comp in range(tpl_ref.shape[0]):
        fill_hankel(ext_ref[ext_at + comp : ext_at + comp + 1, :], hankel_ref.at[comp])
    lhs = [lag_rows(tpl_ref[comp].astype(F32), rows, length) for comp in range(tpl_ref.shape[0])]
    for comp in range(tpl_ref.shape[0]):
        rhs = jnp.concatenate(
            [hankel_ref[comp, :, :reach], hankel_ref[comp, :, LANES : LANES + reach]], axis=0
        )
        product_ref[comp] = jnp.dot(lhs[comp], rhs, preferred_element_type=F32)


def collect(inv_at, rows, comps, inv_ref, acc_refs, work_refs, spans):
    product_ref = work_refs[1]
    splits = product_ref.shape[1] // rows
    for start, size, store in spans:
        chunk = None
        for ref in acc_refs:
            part = ref[:, pl.ds(start, size)]
            chunk = part if chunk is None else chunk + part
        for comp in range(comps):
            part = product_ref[comp, :rows, pl.ds(start, size)]
            for split in range(1, splits):
                shift = split * 2 * LANES
                part = part + product_ref[comp, split * rows : (split + 1) * rows, pl.ds(start + shift, size)]
            part = part * inv_ref[inv_at + comp : inv_at + comp + 1, pl.ds(start, size)]
            chunk = part if chunk is None else chunk + part
        store(chunk)


def spans_of(total, store):
    return [
        (start, min(CHUNK, total - start), functools.partial(store, start)) for start in range(0, total, CHUNK)
    ]


def storing(ref):
    def store(start, chunk):
        ref[:, start : start + chunk.shape[1]] = chunk

    return store


def correlate(at, rows, length, tpl_ref, ext_ref, inv_ref, acc_refs, work_refs, store):
    multiply(at, rows, length, tpl_ref, ext_ref, work_refs)
    spans = spans_of(inv_ref.shape[-1], store)
    collect(at, rows, tpl_ref.shape[0], inv_ref, acc_refs, work_refs, spans)


def first_kernel(shards, chips, rows, length, halo, crossing, tpl_ref, *refs):
    shard_refs, tail_refs = refs[:shards], refs[shards : shards + chips]
    ext_ref, inv_ref, cross_ref, sum_ref, both_ref, *work_refs = refs[shards + chips :]
    comps, total = tpl_ref.shape[0], inv_ref.shape[-1]
    fill_samples(halo, lax.axis_index("tm"), shard_refs, tail_refs, ext_ref)
    multiply(0, rows, length, tpl_ref, ext_ref, work_refs)
    fill_inverse(length, ext_ref, both_ref, inv_ref)
    cross_ref[:comps, :] = ext_ref[crossing * comps : (crossing + 1) * comps, :]
    cross_ref[comps:, :total] = inv_ref[crossing * comps : (crossing + 1) * comps, :]
    cross_ref[comps:, total:] = jnp.zeros((comps, cross_ref.shape[-1] - total), F32)
    collect(0, rows, comps, inv_ref, [], work_refs, spans_of(total, storing(sum_ref)))


def middle_kernel(at, rows, length, tpl_ref, ext_ref, inv_ref, acc_ref, sum_ref, *work_refs):
    correlate(at, rows, length, tpl_ref, ext_ref, inv_ref, [acc_ref], work_refs, storing(sum_ref))


def parting_kernel(at, rows, length, tpl_ref, ext_ref, inv_ref, acc_ref, keep_ref, early_ref, late_ref, *work_refs):
    own = rows // 2
    low = lax.axis_index("sta") % 2 == 0
    middle = early_ref.shape[-1]

    def store(start, chunk):
        stop = start + chunk.shape[1]
        keep_ref[:, start:stop] = jnp.where(low, chunk[:own], chunk[own:])
        send = jnp.where(low, chunk[own:], chunk[:own]).astype(BF16)
        if start < middle:
            early_ref[:, start : min(stop, middle)] = send[:, : min(stop, middle) - start]
        if stop > middle:
            late_ref[:, max(start, middle) - middle : stop - middle] = send[:, max(start, middle) - start :]

    correlate(at, rows, length, tpl_ref, ext_ref, inv_ref, [acc_ref], work_refs, store)


def closing_kernel(shards, rows, length, tpl_ref, cross_ref, acc_ref, early_ref, late_ref, *refs):
    out_refs, (sum_ref, *work_refs) = refs[:shards], refs[shards:]
    comps, middle = tpl_ref.shape[0], early_ref.shape[-1]
    sum_ref[:, :middle] = acc_ref[:, :middle] + early_ref[...].astype(F32)
    sum_ref[:, middle:] = acc_ref[:, middle:] + late_ref[...].astype(F32)
    multiply(0, rows, length, tpl_ref, cross_ref, work_refs)
    samples = out_refs[0].shape[-1]
    tm_index = lax.axis_index("tm")

    def storing_in(ref):
        def store(chunk):
            chunk = chunk.astype(ref.dtype)
            if ref.shape[0] > rows:
                more = jnp.zeros((ref.shape[0] - rows, samples), ref.dtype)
                chunk = jnp.concatenate([chunk, more], axis=0)
            ref[...] = chunk

        return store

    spans = [
        (pl.multiple_of((tm_index ^ offset) * samples, LANES), samples, storing_in(ref))
        for offset, ref in enumerate(out_refs)
    ]
    collect(comps, rows, comps, cross_ref, [sum_ref], work_refs, spans)


def work_buffers(comps, rows, total, width, length):
    splits = -(-length // (2 * LANES))
    reach = total + (splits - 1) * 2 * LANES
    return [pltpu.VMEM((comps, LANES, width), BF16), pltpu.VMEM((comps, splits * rows, reach), F32)]


def first(rows, length, halo, crossing, tpl, shards, tails):
    chips, comps, samples = shards[0].shape
    total = samples * len(shards)
    width = total + up(length, LANES)
    count = chips * comps
    return pl.pallas_call(
        functools.partial(first_kernel, len(shards), chips, rows, length, halo, crossing),
        out_shape=[
            jax.ShapeDtypeStruct((count, width), F32),
            jax.ShapeDtypeStruct((count, total), F32),
            jax.ShapeDtypeStruct((2 * comps, width), F32),
            jax.ShapeDtypeStruct((rows, total), F32),
        ],
        in_specs=[VMEM] * (1 + len(shards) + chips),
        out_specs=[VMEM] * 4,
        scratch_shapes=[pltpu.VMEM((up(2 * count, 8), width), F32)]
        + work_buffers(comps, rows, total, width, length),
        compiler_params=params(24),
        cost_estimate=CHEAP,
    )(tpl, *shards, *tails)


def later(kernel, rows, total, length, out_shape, inputs, scratch=(), flops=1):
    comps, width = inputs[0].shape[0], inputs[1].shape[-1]
    return pl.pallas_call(
        kernel,
        out_shape=out_shape,
        in_specs=[VMEM] * len(inputs),
        out_specs=[VMEM] * len(out_shape),
        scratch_shapes=list(scratch) + work_buffers(comps, rows, total, width, length),
        compiler_params=params(24),
        cost_estimate=pl.CostEstimate(flops=flops, bytes_accessed=1, transcendentals=0),
    )(*inputs)


def gather_kernel(*refs):
    *part_refs, out_ref, held_ref, left = refs
    tm_index = lax.axis_index("tm")
    copies = []
    for offset, ref in enumerate(part_refs):
        held_ref[offset] = ref[: out_ref.shape[1], :].astype(F32)
        copies.append(
            pltpu.make_async_copy(held_ref.at[offset], out_ref.at[tm_index ^ offset], left.at[offset])
        )
        copies[-1].start()
    for copy in copies:
        copy.wait()


def gather(parts):
    shape = (len(parts),) + parts[0].shape
    return pl.pallas_call(
        gather_kernel,
        out_shape=jax.ShapeDtypeStruct(shape, F32),
        in_specs=[VMEM] * len(parts),
        out_specs=HBM,
        scratch_shapes=[pltpu.VMEM(shape, F32), pltpu.SemaphoreType.DMA((len(parts),))],
        compiler_params=params(16),
    )(*parts)


def per_device(templates, channel_mask, waveforms, waveform_tail):
    length = templates.shape[-1]
    samples = waveforms.shape[-1]
    halo = waveform_tail.shape[-1]
    tm_count = lax.axis_size("tm")
    chips = lax.axis_size("sta") // 2
    tpl = jnp.transpose(templates[0, :, 0], (1, 2, 0))
    mask = channel_mask[..., 0]
    rows = tpl.shape[-1] // chips
    own = rows // 2
    total = samples * tm_count
    comps = tpl.shape[0]
    final = chips // 2
    between = [1] + [offset for offset in range(chips - 1, 1, -1) if offset != final]

    wave = join(waveforms[0], waveform_tail[0])
    waves = [wave] + [swap_with(wave, "sta", 2 * offset) for offset in range(1, chips)]
    offsets = [0] + between
    targets = [(offset, None) for offset in offsets] + [(final, 0), (final, 1)]
    messages = pack(targets, [rows] * len(offsets) + [own] * 2, tpl, mask)
    messages, waves = lax.optimization_barrier((messages, waves))
    pieces = {offset: swap_with(messages[1 + i], "sta", 2 * offset) for i, offset in enumerate(between)}
    stacked = jnp.stack([part[:, :samples] for part in waves])
    shards = [stacked] + [swap_with(stacked, "tm", offset) for offset in range(1, tm_count)]
    late = [None, None]
    late[0], shards[-1] = lax.optimization_barrier((messages[-2], shards[-1]))
    late[1], shards[-2] = lax.optimization_barrier((messages[-1], shards[-2]))
    straight = swap_with(late[0], "sta", 2 * final)
    crossed = swap_with(late[1], "sta", 2 * final + 1)
    ext, inv, cross, acc = first(rows, length, halo, final, messages[0], shards, waves)
    cross = swap_with(cross, "sta", 1)
    whole = jax.ShapeDtypeStruct((rows, total), F32)
    for offset in between[:-1]:
        kernel = functools.partial(middle_kernel, offset * comps, rows, length)
        (acc,) = later(kernel, rows, total, length, [whole], [pieces[offset], ext, inv, acc], flops=F_MID)
    middle = up(total // 2, LANES)
    half = jax.ShapeDtypeStruct((own, total), F32)
    halves = [jax.ShapeDtypeStruct((own, size), BF16) for size in (middle, total - middle)]
    kernel = functools.partial(parting_kernel, between[-1] * comps, rows, length)
    inputs = [pieces[between[-1]], ext, inv, acc]
    keep, *send = later(kernel, rows, total, length, [half] + halves, inputs, flops=F_PART)
    came = [swap_with(part, "sta", 1) for part in send]
    kernel = functools.partial(middle_kernel, final * comps, own, length)
    (acc,) = later(kernel, own, total, length, [half], [straight, ext, inv, keep], flops=F_JOIN)
    kernel = functools.partial(closing_kernel, tm_count, own, length)
    parts = [jax.ShapeDtypeStruct((own, samples), F32)] + [
        jax.ShapeDtypeStruct((own + (EXTRA if offset & (offset - 1) else 0), samples), BF16)
        for offset in range(1, tm_count)
    ]
    inputs = [crossed, cross, acc, *came]
    parts = later(kernel, own, total, length, parts, inputs, [pltpu.VMEM((own, total), F32)], F_CLOSE)
    parts = [parts[0]] + [swap_with(parts[offset], "tm", offset) for offset in range(1, tm_count)]
    return gather(parts)


def solution(mesh):
    placed = (
        P("tm", None, "sta", None, None),
        P("tm", None, "sta"),
        P("sta", None, "tm"),
        P("sta", None, None),
    )
    return jax.shard_map(
        per_device, mesh=mesh, in_specs=placed, out_specs=P(None, "sta", "tm"), check_vma=False
    )
```

```python
import functools
import jax
import jax.numpy as jnp
from jax import lax
from jax.experimental import pallas as pl
from jax.experimental.pallas import tpu as pltpu
from jax.sharding import PartitionSpec as P

F32 = jnp.float32
BF16 = jnp.bfloat16
LANES = 128
CHUNK = 512
EXTRA = 128
VMEM = pl.BlockSpec(memory_space=pltpu.VMEM)
HBM = pl.BlockSpec(memory_space=pltpu.HBM)
F_MID, F_PART, F_JOIN, F_CLOSE = 500000000, 1, 500000000, 1
CHEAP = pl.CostEstimate(flops=1, bytes_accessed=1, transcendentals=0)


def params(limit_mib):
    return pltpu.CompilerParams(vmem_limit_bytes=limit_mib << 20)


def up(value, multiple):
    return (value + multiple - 1) // multiple * multiple


def swap_with(x, axis, offset):
    size = lax.axis_size(axis)
    return lax.ppermute(x, axis, [(i, i ^ offset) for i in range(size)])


def join_kernel(wave_ref, tail_ref, tpl_ref, mask_ref, out_ref, tpl_out, mask_out, wave_held, tail_held, arrived):
    pairs = ((wave_ref, wave_held), (tail_ref, tail_held), (mask_ref, mask_out), (tpl_ref, tpl_out))
    copies = [pltpu.make_async_copy(source, held, arrived.at[i]) for i, (source, held) in enumerate(pairs)]
    for copy in copies:
        copy.start()
    copies[0].wait()
    copies[1].wait()
    samples = wave_held.shape[-1]
    out_ref[...] = jnp.zeros_like(out_ref)
    out_ref[:, :samples] = wave_held[...]
    out_ref[:, samples : samples + tail_held.shape[-1]] = tail_held[...]
    copies[2].wait()
    copies[3].wait()


def join(wave, tail, tpl, mask):
    inputs = (wave, tail, tpl, mask)
    return pl.pallas_call(
        join_kernel,
        out_shape=[
            jax.ShapeDtypeStruct((wave.shape[0], up(wave.shape[-1] + tail.shape[-1], LANES)), BF16),
            jax.ShapeDtypeStruct(tpl.shape, tpl.dtype),
            jax.ShapeDtypeStruct(mask.shape, mask.dtype),
        ],
        in_specs=[HBM] * 4,
        out_specs=[VMEM] * 3,
        scratch_shapes=[pltpu.VMEM(x.shape, x.dtype) for x in (wave, tail)] + [pltpu.SemaphoreType.DMA((4,))],
        compiler_params=params(16),
        cost_estimate=CHEAP,
    )(*[pltpu.with_memory_space_constraint(x, pltpu.HBM) for x in inputs])


def first_row(chip_offset, core_offset, all_rows):
    index = lax.axis_index("sta")
    rows = all_rows // (lax.axis_size("sta") // 2)
    row = (index // 2 ^ chip_offset) * rows
    return row if core_offset is None else row + (index % 2 ^ core_offset) * (rows // 2)


def fold_lags(rows, length):
    return up(-(-length // (LANES // rows)), 8)


def pack_kernel(targets, counts, length, tpl_ref, mask_ref, *tpl_outs):
    lane = lax.broadcasted_iota(jnp.int32, (1, LANES), 1)
    for target, rows, out_ref in zip(targets, counts, tpl_outs):
        lags = fold_lags(rows, length)
        row = first_row(*target, tpl_ref.shape[-1])
        tile = pl.multiple_of(row // LANES * LANES, LANES)
        mask = mask_ref[:, pl.ds(tile, LANES)].astype(F32)
        for comp in range(tpl_ref.shape[0]):
            values = tpl_ref[comp, :, pl.ds(tile, LANES)].astype(F32) * mask
            folded = jnp.zeros((lags, LANES), F32)
            for fold in range(LANES // rows):
                piece = values[fold * lags : min((fold + 1) * lags, length)]
                if piece.shape[0] == 0:
                    continue
                if piece.shape[0] < lags:
                    piece = jnp.concatenate([piece, jnp.zeros((lags - piece.shape[0], LANES), F32)], axis=0)
                turned = pltpu.roll(piece, (fold * rows - row % LANES + LANES) % LANES, 1)
                here = (lane >= fold * rows) & (lane < (fold + 1) * rows)
                folded = jnp.where(here, turned, folded)
            out_ref[comp] = folded.astype(BF16)


def pack(targets, counts, tpl, mask):
    comps, length, _ = tpl.shape
    return pl.pallas_call(
        functools.partial(pack_kernel, targets, counts, length),
        out_shape=[jax.ShapeDtypeStruct((comps, fold_lags(rows, length), LANES), BF16) for rows in counts],
        in_specs=[VMEM] * 2,
        out_specs=[VMEM] * len(counts),
        compiler_params=params(16),
        cost_estimate=CHEAP,
    )(tpl, mask)


def fill_samples(halo, tm_index, shard_refs, tail_refs, ext_ref):
    chips, comps, samples = shard_refs[0].shape
    total = samples * len(shard_refs)
    ext_ref[...] = jnp.zeros_like(ext_ref)
    for chip in range(chips):
        at = chip * comps
        for offset, ref in enumerate(shard_refs):
            start = pl.multiple_of((tm_index ^ offset) * samples, LANES)
            ext_ref[at : at + comps, pl.ds(start, samples)] = ref[chip].astype(F32)
        ext_ref[at : at + comps, total : total + halo] = tail_refs[chip][:, samples : samples + halo].astype(F32)


def fill_inverse(length, ext_ref, both_ref, inv_ref):
    count, width = ext_ref.shape
    total = inv_ref.shape[-1]
    both_ref[:count, :] = ext_ref[...]
    both_ref[count : 2 * count, :] = ext_ref[...] * ext_ref[...]
    result, done, span, doubled = None, 0, 1, both_ref[: 2 * count, :]
    while span <= length:
        if length & span:
            part = doubled if done == 0 else pltpu.roll(doubled, width - done, 1)
            result = part if result is None else result + part
            done += span
        span *= 2
        if span <= length:
            doubled = doubled + pltpu.roll(doubled, width - span // 2, 1)
    both_ref[: 2 * count, :] = result
    window_sum = both_ref[:count, :total]
    window_square = both_ref[count : 2 * count, :total]
    inv_ref[...] = lax.rsqrt(window_square - window_sum * window_sum / length + 1e-05)


def lag_rows(values, rows, length):
    lags = values.shape[0]
    folds = LANES // rows
    splits = -(-length // (2 * LANES))

    def over_folds(total):
        span = rows
        while span < LANES:
            total = total + pltpu.roll(total, span, 1)
            span *= 2
        return total

    lane = lax.broadcasted_iota(jnp.int32, values.shape, 1)
    lag = lax.broadcasted_iota(jnp.int32, values.shape, 0) + lane // rows * lags
    mean = over_folds(jnp.sum(values, axis=0, keepdims=True)) / length
    centred = jnp.where(lag < length, values - mean, 0.0)
    energy = over_folds(jnp.sum(centred * centred, axis=0, keepdims=True))
    weighted = centred * lax.rsqrt(energy + 1e-05)
    parts = [weighted] + [pltpu.roll(weighted, LANES - fold * rows, 1) for fold in range(1, folds)]
    wanted = splits * 2 * LANES
    if folds * lags < wanted:
        parts.append(jnp.zeros((wanted - folds * lags, LANES), F32))
    spread = jnp.concatenate(parts, axis=0)
    low = lax.broadcasted_iota(jnp.int32, (LANES, LANES), 1) < LANES // 2
    flip = (
        lax.broadcasted_iota(jnp.int32, (LANES, LANES), 0)
        + lax.broadcasted_iota(jnp.int32, (LANES, LANES), 1)
        == LANES - 1
    ).astype(BF16)
    result = []
    for split in range(splits):
        at = split * 2 * LANES
        both = jnp.where(low, spread[at : at + LANES], pltpu.roll(spread[at + LANES : at + 2 * LANES], LANES // 2, 1))
        turned = lax.dot_general(
            both.astype(BF16), flip, (((0,), (0,)), ((), ())), preferred_element_type=F32
        )
        result.append(jnp.concatenate([turned[:rows], turned[LANES // 2 : LANES // 2 + rows]], axis=1))
    return jnp.concatenate(result, axis=0).astype(BF16)


def fill_hankel(row, out_ref):
    width = row.shape[-1]
    spread = jnp.broadcast_to(row.astype(BF16), (LANES, width))
    out_ref[...] = pltpu.roll(spread, width - (LANES - 1), 1, stride=1, stride_axis=0)


def multiply(ext_at, rows, length, tpl_ref, ext_ref, work_refs):
    hankel_ref, product_ref = work_refs
    reach = product_ref.shape[-1]
    for comp in range(tpl_ref.shape[0]):
        fill_hankel(ext_ref[ext_at + comp : ext_at + comp + 1, :], hankel_ref.at[comp])
    lhs = [lag_rows(tpl_ref[comp].astype(F32), rows, length) for comp in range(tpl_ref.shape[0])]
    for comp in range(tpl_ref.shape[0]):
        rhs = jnp.concatenate(
            [hankel_ref[comp, :, :reach], hankel_ref[comp, :, LANES : LANES + reach]], axis=0
        )
        product_ref[comp] = jnp.dot(lhs[comp], rhs, preferred_element_type=F32)


def collect(inv_at, rows, comps, inv_ref, acc_refs, work_refs, spans):
    product_ref = work_refs[1]
    splits = product_ref.shape[1] // rows
    for start, size, store in spans:
        chunk = None
        for ref in acc_refs:
            part = ref[:, pl.ds(start, size)]
            chunk = part if chunk is None else chunk + part
        for comp in range(comps):
            part = product_ref[comp, :rows, pl.ds(start, size)]
            for split in range(1, splits):
                shift = split * 2 * LANES
                part = part + product_ref[comp, split * rows : (split + 1) * rows, pl.ds(start + shift, size)]
            part = part * inv_ref[inv_at + comp : inv_at + comp + 1, pl.ds(start, size)]
            chunk = part if chunk is None else chunk + part
        store(chunk)


def spans_of(total, store):
    return [
        (start, min(CHUNK, total - start), functools.partial(store, start)) for start in range(0, total, CHUNK)
    ]


def storing(ref):
    def store(start, chunk):
        ref[:, start : start + chunk.shape[1]] = chunk

    return store


def correlate(at, rows, length, tpl_ref, ext_ref, inv_ref, acc_refs, work_refs, store):
    multiply(at, rows, length, tpl_ref, ext_ref, work_refs)
    spans = spans_of(inv_ref.shape[-1], store)
    collect(at, rows, tpl_ref.shape[0], inv_ref, acc_refs, work_refs, spans)


def first_kernel(shards, chips, rows, length, halo, crossing, tpl_ref, *refs):
    shard_refs, tail_refs = refs[:shards], refs[shards : shards + chips]
    ext_ref, inv_ref, cross_ref, sum_ref, both_ref, *work_refs = refs[shards + chips :]
    comps, total = tpl_ref.shape[0], inv_ref.shape[-1]
    fill_samples(halo, lax.axis_index("tm"), shard_refs, tail_refs, ext_ref)
    multiply(0, rows, length, tpl_ref, ext_ref, work_refs)
    fill_inverse(length, ext_ref, both_ref, inv_ref)
    cross_ref[:comps, :] = ext_ref[crossing * comps : (crossing + 1) * comps, :]
    cross_ref[comps:, :total] = inv_ref[crossing * comps : (crossing + 1) * comps, :]
    cross_ref[comps:, total:] = jnp.zeros((comps, cross_ref.shape[-1] - total), F32)
    collect(0, rows, comps, inv_ref, [], work_refs, spans_of(total, storing(sum_ref)))


def middle_kernel(at, rows, length, tpl_ref, ext_ref, inv_ref, acc_ref, sum_ref, *work_refs):
    correlate(at, rows, length, tpl_ref, ext_ref, inv_ref, [acc_ref], work_refs, storing(sum_ref))


def parting_kernel(at, rows, length, tpl_ref, ext_ref, inv_ref, acc_ref, keep_ref, early_ref, late_ref, *work_refs):
    own = rows // 2
    low = lax.axis_index("sta") % 2 == 0
    middle = early_ref.shape[-1]

    def store(start, chunk):
        stop = start + chunk.shape[1]
        keep_ref[:, start:stop] = jnp.where(low, chunk[:own], chunk[own:])
        send = jnp.where(low, chunk[own:], chunk[:own]).astype(BF16)
        if start < middle:
            early_ref[:, start : min(stop, middle)] = send[:, : min(stop, middle) - start]
        if stop > middle:
            late_ref[:, max(start, middle) - middle : stop - middle] = send[:, max(start, middle) - start :]

    correlate(at, rows, length, tpl_ref, ext_ref, inv_ref, [acc_ref], work_refs, store)


def closing_kernel(shards, rows, length, tpl_ref, cross_ref, acc_ref, early_ref, late_ref, *refs):
    out_refs, (sum_ref, *work_refs) = refs[:shards], refs[shards:]
    comps, middle = tpl_ref.shape[0], early_ref.shape[-1]
    sum_ref[:, :middle] = acc_ref[:, :middle] + early_ref[...].astype(F32)
    sum_ref[:, middle:] = acc_ref[:, middle:] + late_ref[...].astype(F32)
    multiply(0, rows, length, tpl_ref, cross_ref, work_refs)
    samples = out_refs[0].shape[-1]
    tm_index = lax.axis_index("tm")

    def storing_in(ref):
        def store(chunk):
            ref[:, :samples] = chunk.astype(ref.dtype)
            if ref.shape[1] > samples:
                ref[:, samples:] = jnp.zeros((rows, ref.shape[1] - samples), ref.dtype)

        return store

    spans = [
        (pl.multiple_of((tm_index ^ offset) * samples, LANES), samples, storing_in(ref))
        for offset, ref in enumerate(out_refs)
    ]
    collect(comps, rows, comps, cross_ref, [sum_ref], work_refs, spans)


def work_buffers(comps, rows, total, width, length):
    splits = -(-length // (2 * LANES))
    reach = total + (splits - 1) * 2 * LANES
    return [pltpu.VMEM((comps, LANES, width), BF16), pltpu.VMEM((comps, splits * rows, reach), F32)]


def first(rows, length, halo, crossing, tpl, shards, tails):
    chips, comps, samples = shards[0].shape
    total = samples * len(shards)
    width = total + up(length, LANES)
    count = chips * comps
    return pl.pallas_call(
        functools.partial(first_kernel, len(shards), chips, rows, length, halo, crossing),
        out_shape=[
            jax.ShapeDtypeStruct((count, width), F32),
            jax.ShapeDtypeStruct((count, total), F32),
            jax.ShapeDtypeStruct((2 * comps, width), F32),
            jax.ShapeDtypeStruct((rows, total), F32),
        ],
        in_specs=[VMEM] * (1 + len(shards) + chips),
        out_specs=[VMEM] * 4,
        scratch_shapes=[pltpu.VMEM((up(2 * count, 8), width), F32)]
        + work_buffers(comps, rows, total, width, length),
        compiler_params=params(24),
        cost_estimate=CHEAP,
    )(tpl, *shards, *tails)


def later(kernel, rows, total, length, out_shape, inputs, scratch=(), flops=1):
    comps, width = inputs[0].shape[0], inputs[1].shape[-1]
    return pl.pallas_call(
        kernel,
        out_shape=out_shape,
        in_specs=[VMEM] * len(inputs),
        out_specs=[VMEM] * len(out_shape),
        scratch_shapes=list(scratch) + work_buffers(comps, rows, total, width, length),
        compiler_params=params(24),
        cost_estimate=pl.CostEstimate(flops=flops, bytes_accessed=1, transcendentals=0),
    )(*inputs)


def gather_kernel(*refs):
    *part_refs, out_ref, held_ref, left = refs
    tm_index = lax.axis_index("tm")
    copies = []
    for offset, ref in enumerate(part_refs):
        held_ref[offset] = ref[:, : out_ref.shape[2]].astype(F32)
        copies.append(
            pltpu.make_async_copy(held_ref.at[offset], out_ref.at[tm_index ^ offset], left.at[offset])
        )
        copies[-1].start()
    for copy in copies:
        copy.wait()


def gather(parts):
    shape = (len(parts),) + parts[0].shape
    return pl.pallas_call(
        gather_kernel,
        out_shape=jax.ShapeDtypeStruct(shape, F32),
        in_specs=[VMEM] * len(parts),
        out_specs=HBM,
        scratch_shapes=[pltpu.VMEM(shape, F32), pltpu.SemaphoreType.DMA((len(parts),))],
        compiler_params=params(16),
    )(*parts)


def per_device(templates, channel_mask, waveforms, waveform_tail):
    length = templates.shape[-1]
    samples = waveforms.shape[-1]
    halo = waveform_tail.shape[-1]
    tm_count = lax.axis_size("tm")
    chips = lax.axis_size("sta") // 2
    tpl = jnp.transpose(templates[0, :, 0], (1, 2, 0))
    mask = channel_mask[..., 0]
    rows = tpl.shape[-1] // chips
    own = rows // 2
    total = samples * tm_count
    comps = tpl.shape[0]
    final = chips // 2
    between = [1] + [offset for offset in range(chips - 1, 1, -1) if offset != final]

    wave, tpl, mask = join(waveforms[0], waveform_tail[0], tpl, mask)
    waves = [wave] + [swap_with(wave, "sta", 2 * offset) for offset in range(1, chips)]
    offsets = [0] + between
    targets = [(offset, None) for offset in offsets] + [(final, 0), (final, 1)]
    messages = pack(targets, [rows] * len(offsets) + [own] * 2, tpl, mask)
    pieces = {offset: swap_with(messages[1 + i], "sta", 2 * offset) for i, offset in enumerate(between)}
    stacked = jnp.stack([part[:, :samples] for part in waves])
    shards = [stacked] + [swap_with(stacked, "tm", offset) for offset in range(1, tm_count)]
    late = [None, None]
    late[0], shards[-1] = lax.optimization_barrier((messages[-2], shards[-1]))
    late[1], shards[-2] = lax.optimization_barrier((messages[-1], shards[-2]))
    straight = swap_with(late[0], "sta", 2 * final)
    crossed = swap_with(late[1], "sta", 2 * final + 1)
    ext, inv, cross, acc = first(rows, length, halo, final, messages[0], shards, waves)
    cross = swap_with(cross, "sta", 1)
    whole = jax.ShapeDtypeStruct((rows, total), F32)
    for offset in between[:-1]:
        kernel = functools.partial(middle_kernel, offset * comps, rows, length)
        (acc,) = later(kernel, rows, total, length, [whole], [pieces[offset], ext, inv, acc], flops=F_MID)
    middle = up(total // 2, LANES)
    half = jax.ShapeDtypeStruct((own, total), F32)
    halves = [jax.ShapeDtypeStruct((own, size), BF16) for size in (middle, total - middle)]
    kernel = functools.partial(parting_kernel, between[-1] * comps, rows, length)
    inputs = [pieces[between[-1]], ext, inv, acc]
    keep, *send = later(kernel, rows, total, length, [half] + halves, inputs, flops=F_PART)
    came = [swap_with(part, "sta", 1) for part in send]
    kernel = functools.partial(middle_kernel, final * comps, own, length)
    (acc,) = later(kernel, own, total, length, [half], [straight, ext, inv, keep], flops=F_JOIN)
    kernel = functools.partial(closing_kernel, tm_count, own, length)
    parts = [jax.ShapeDtypeStruct((own, samples), F32)] + [
        jax.ShapeDtypeStruct((own, samples + (EXTRA if offset & (offset - 1) else 0)), BF16)
        for offset in range(1, tm_count)
    ]
    inputs = [crossed, cross, acc, *came]
    parts = later(kernel, own, total, length, parts, inputs, [pltpu.VMEM((own, total), F32)], F_CLOSE)
    parts = [parts[0]] + [swap_with(parts[offset], "tm", offset) for offset in range(1, tm_count)]
    return gather(parts)


def solution(mesh):
    placed = (
        P("tm", None, "sta", None, None),
        P("tm", None, "sta"),
        P("sta", None, "tm"),
        P("sta", None, None),
    )
    return jax.shard_map(
        per_device, mesh=mesh, in_specs=placed, out_specs=P(None, "sta", "tm"), check_vma=False
    )
```

```python
import functools
import jax
import jax.numpy as jnp
from jax import lax
from jax.experimental import pallas as pl
from jax.experimental.pallas import tpu as pltpu
from jax.sharding import PartitionSpec as P

F32 = jnp.float32
BF16 = jnp.bfloat16
LANES = 128
CHUNK = 512
EXTRA = 128
VMEM = pl.BlockSpec(memory_space=pltpu.VMEM)
HBM = pl.BlockSpec(memory_space=pltpu.HBM)
F_MID, F_PART, F_JOIN, F_CLOSE = 500000000, 1, 500000000, 1
CHEAP = pl.CostEstimate(flops=1, bytes_accessed=1, transcendentals=0)


def params(limit_mib):
    return pltpu.CompilerParams(vmem_limit_bytes=limit_mib << 20)


def up(value, multiple):
    return (value + multiple - 1) // multiple * multiple


def swap_with(x, axis, offset):
    size = lax.axis_size(axis)
    return lax.ppermute(x, axis, [(i, i ^ offset) for i in range(size)])


def join_kernel(wave_ref, tail_ref, tpl_ref, mask_ref, out_ref, tpl_out, mask_out, wave_held, tail_held, arrived):
    pairs = ((wave_ref, wave_held), (tail_ref, tail_held), (mask_ref, mask_out), (tpl_ref, tpl_out))
    copies = [pltpu.make_async_copy(source, held, arrived.at[i]) for i, (source, held) in enumerate(pairs)]
    for copy in copies:
        copy.start()
    copies[0].wait()
    copies[1].wait()
    samples = wave_held.shape[-1]
    out_ref[...] = jnp.zeros_like(out_ref)
    out_ref[:, :samples] = wave_held[...]
    out_ref[:, samples : samples + tail_held.shape[-1]] = tail_held[...]
    copies[2].wait()
    copies[3].wait()


def join(wave, tail, tpl, mask):
    inputs = (wave, tail, tpl, mask)
    return pl.pallas_call(
        join_kernel,
        out_shape=[
            jax.ShapeDtypeStruct((wave.shape[0], up(wave.shape[-1] + tail.shape[-1], LANES)), BF16),
            jax.ShapeDtypeStruct(tpl.shape, tpl.dtype),
            jax.ShapeDtypeStruct(mask.shape, mask.dtype),
        ],
        in_specs=[HBM] * 4,
        out_specs=[VMEM] * 3,
        scratch_shapes=[pltpu.VMEM(x.shape, x.dtype) for x in (wave, tail)] + [pltpu.SemaphoreType.DMA((4,))],
        compiler_params=params(16),
        cost_estimate=CHEAP,
    )(*[pltpu.with_memory_space_constraint(x, pltpu.HBM) for x in inputs])


def first_row(chip_offset, core_offset, all_rows):
    index = lax.axis_index("sta")
    rows = all_rows // (lax.axis_size("sta") // 2)
    row = (index // 2 ^ chip_offset) * rows
    return row if core_offset is None else row + (index % 2 ^ core_offset) * (rows // 2)


def fold_lags(rows, length):
    return up(-(-length // (LANES // rows)), 8)


def pack_kernel(targets, counts, length, tpl_ref, mask_ref, *tpl_outs):
    lane = lax.broadcasted_iota(jnp.int32, (1, LANES), 1)
    for target, rows, out_ref in zip(targets, counts, tpl_outs):
        lags = fold_lags(rows, length)
        row = first_row(*target, tpl_ref.shape[-1])
        tile = pl.multiple_of(row // LANES * LANES, LANES)
        mask = mask_ref[:, pl.ds(tile, LANES)].astype(F32)
        for comp in range(tpl_ref.shape[0]):
            values = tpl_ref[comp, :, pl.ds(tile, LANES)].astype(F32) * mask
            folded = jnp.zeros((lags, LANES), F32)
            for fold in range(LANES // rows):
                piece = values[fold * lags : min((fold + 1) * lags, length)]
                if piece.shape[0] == 0:
                    continue
                if piece.shape[0] < lags:
                    piece = jnp.concatenate([piece, jnp.zeros((lags - piece.shape[0], LANES), F32)], axis=0)
                turned = pltpu.roll(piece, (fold * rows - row % LANES + LANES) % LANES, 1)
                here = (lane >= fold * rows) & (lane < (fold + 1) * rows)
                folded = jnp.where(here, turned, folded)
            out_ref[comp] = folded.astype(BF16)


def pack(targets, counts, tpl, mask):
    comps, length, _ = tpl.shape
    return pl.pallas_call(
        functools.partial(pack_kernel, targets, counts, length),
        out_shape=[jax.ShapeDtypeStruct((comps, fold_lags(rows, length), LANES), BF16) for rows in counts],
        in_specs=[VMEM] * 2,
        out_specs=[VMEM] * len(counts),
        compiler_params=params(16),
        cost_estimate=CHEAP,
    )(tpl, mask)


def fill_samples(halo, tm_index, shard_refs, tail_refs, ext_ref):
    chips, comps, samples = shard_refs[0].shape
    total = samples * len(shard_refs)
    ext_ref[...] = jnp.zeros_like(ext_ref)
    for chip in range(chips):
        at = chip * comps
        for offset, ref in enumerate(shard_refs):
            start = pl.multiple_of((tm_index ^ offset) * samples, LANES)
            ext_ref[at : at + comps, pl.ds(start, samples)] = ref[chip].astype(F32)
        ext_ref[at : at + comps, total : total + halo] = tail_refs[chip][:, samples : samples + halo].astype(F32)


def fill_inverse(length, ext_ref, both_ref, inv_ref):
    count, width = ext_ref.shape
    total = inv_ref.shape[-1]
    both_ref[:count, :] = ext_ref[...]
    both_ref[count : 2 * count, :] = ext_ref[...] * ext_ref[...]
    result, done, span, doubled = None, 0, 1, both_ref[: 2 * count, :]
    while span <= length:
        if length & span:
            part = doubled if done == 0 else pltpu.roll(doubled, width - done, 1)
            result = part if result is None else result + part
            done += span
        span *= 2
        if span <= length:
            doubled = doubled + pltpu.roll(doubled, width - span // 2, 1)
    both_ref[: 2 * count, :] = result
    window_sum = both_ref[:count, :total]
    window_square = both_ref[count : 2 * count, :total]
    inv_ref[...] = lax.rsqrt(window_square - window_sum * window_sum / length + 1e-05)


def lag_rows(values, rows, length):
    lags = values.shape[0]
    folds = LANES // rows
    splits = -(-length // (2 * LANES))

    def over_folds(total):
        span = rows
        while span < LANES:
            total = total + pltpu.roll(total, span, 1)
            span *= 2
        return total

    lane = lax.broadcasted_iota(jnp.int32, values.shape, 1)
    lag = lax.broadcasted_iota(jnp.int32, values.shape, 0) + lane // rows * lags
    mean = over_folds(jnp.sum(values, axis=0, keepdims=True)) / length
    centred = jnp.where(lag < length, values - mean, 0.0)
    energy = over_folds(jnp.sum(centred * centred, axis=0, keepdims=True))
    weighted = centred * lax.rsqrt(energy + 1e-05)
    parts = [weighted] + [pltpu.roll(weighted, LANES - fold * rows, 1) for fold in range(1, folds)]
    wanted = splits * 2 * LANES
    if folds * lags < wanted:
        parts.append(jnp.zeros((wanted - folds * lags, LANES), F32))
    spread = jnp.concatenate(parts, axis=0)
    low = lax.broadcasted_iota(jnp.int32, (LANES, LANES), 1) < LANES // 2
    flip = (
        lax.broadcasted_iota(jnp.int32, (LANES, LANES), 0)
        + lax.broadcasted_iota(jnp.int32, (LANES, LANES), 1)
        == LANES - 1
    ).astype(BF16)
    result = []
    for split in range(splits):
        at = split * 2 * LANES
        both = jnp.where(low, spread[at : at + LANES], pltpu.roll(spread[at + LANES : at + 2 * LANES], LANES // 2, 1))
        turned = lax.dot_general(
            both.astype(BF16), flip, (((0,), (0,)), ((), ())), preferred_element_type=F32
        )
        result.append(jnp.concatenate([turned[:rows], turned[LANES // 2 : LANES // 2 + rows]], axis=1))
    return jnp.concatenate(result, axis=0).astype(BF16)


def fill_hankel(row, out_ref):
    width = row.shape[-1]
    spread = jnp.broadcast_to(row.astype(BF16), (LANES, width))
    out_ref[...] = pltpu.roll(spread, width - (LANES - 1), 1, stride=1, stride_axis=0)


def multiply(ext_at, rows, length, tpl_ref, ext_ref, work_refs, between=None):
    hankel_ref, product_ref = work_refs
    reach = product_ref.shape[-1]
    comps = tpl_ref.shape[0]
    for comp in range(comps):
        fill_hankel(ext_ref[ext_at + comp : ext_at + comp + 1, :], hankel_ref.at[comp])
    lhs = [lag_rows(tpl_ref[comp].astype(F32), rows, length) for comp in range(comps)]
    for comp in range(comps):
        if comp == comps - 1 and between is not None:
            between()
        rhs = jnp.concatenate(
            [hankel_ref[comp, :, :reach], hankel_ref[comp, :, LANES : LANES + reach]], axis=0
        )
        product_ref[comp] = jnp.dot(lhs[comp], rhs, preferred_element_type=F32)


def collect(inv_at, rows, comps, inv_ref, acc_refs, work_refs, spans):
    product_ref = work_refs[1]
    splits = product_ref.shape[1] // rows
    for start, size, store in spans:
        chunk = None
        for ref in acc_refs:
            part = ref[:, pl.ds(start, size)]
            chunk = part if chunk is None else chunk + part
        for comp in comps:
            part = product_ref[comp, :rows, pl.ds(start, size)]
            for split in range(1, splits):
                shift = split * 2 * LANES
                part = part + product_ref[comp, split * rows : (split + 1) * rows, pl.ds(start + shift, size)]
            part = part * inv_ref[inv_at + comp : inv_at + comp + 1, pl.ds(start, size)]
            chunk = part if chunk is None else chunk + part
        store(chunk)


def spans_of(total, store):
    return [
        (start, min(CHUNK, total - start), functools.partial(store, start)) for start in range(0, total, CHUNK)
    ]


def storing(ref):
    def store(start, chunk):
        ref[:, start : start + chunk.shape[1]] = chunk

    return store


def correlate(at, rows, length, tpl_ref, ext_ref, inv_ref, acc_refs, work_refs, store):
    multiply(at, rows, length, tpl_ref, ext_ref, work_refs)
    spans = spans_of(inv_ref.shape[-1], store)
    collect(at, rows, range(tpl_ref.shape[0]), inv_ref, acc_refs, work_refs, spans)


def first_kernel(shards, chips, rows, length, halo, crossing, tpl_ref, *refs):
    shard_refs, tail_refs = refs[:shards], refs[shards : shards + chips]
    ext_ref, inv_ref, cross_ref, sum_ref, both_ref, *work_refs = refs[shards + chips :]
    comps, total = tpl_ref.shape[0], inv_ref.shape[-1]
    fill_samples(halo, lax.axis_index("tm"), shard_refs, tail_refs, ext_ref)
    multiply(0, rows, length, tpl_ref, ext_ref, work_refs)
    fill_inverse(length, ext_ref, both_ref, inv_ref)
    cross_ref[:comps, :] = ext_ref[crossing * comps : (crossing + 1) * comps, :]
    cross_ref[comps:, :total] = inv_ref[crossing * comps : (crossing + 1) * comps, :]
    cross_ref[comps:, total:] = jnp.zeros((comps, cross_ref.shape[-1] - total), F32)
    collect(0, rows, range(comps), inv_ref, [], work_refs, spans_of(total, storing(sum_ref)))


def middle_kernel(at, rows, length, tpl_ref, ext_ref, inv_ref, acc_ref, sum_ref, *work_refs):
    correlate(at, rows, length, tpl_ref, ext_ref, inv_ref, [acc_ref], work_refs, storing(sum_ref))


def parting_kernel(at, rows, length, tpl_ref, ext_ref, inv_ref, acc_ref, keep_ref, early_ref, late_ref, *work_refs):
    own = rows // 2
    low = lax.axis_index("sta") % 2 == 0
    middle = early_ref.shape[-1]

    def store(start, chunk):
        stop = start + chunk.shape[1]
        keep_ref[:, start:stop] = jnp.where(low, chunk[:own], chunk[own:])
        send = jnp.where(low, chunk[own:], chunk[:own]).astype(BF16)
        if start < middle:
            early_ref[:, start : min(stop, middle)] = send[:, : min(stop, middle) - start]
        if stop > middle:
            late_ref[:, max(start, middle) - middle : stop - middle] = send[:, max(start, middle) - start :]

    correlate(at, rows, length, tpl_ref, ext_ref, inv_ref, [acc_ref], work_refs, store)


def closing_kernel(shards, rows, length, tpl_ref, cross_ref, acc_ref, early_ref, late_ref, *refs):
    out_refs, (sum_ref, *work_refs) = refs[:shards], refs[shards:]
    comps, middle = tpl_ref.shape[0], early_ref.shape[-1]
    sum_ref[:, :middle] = acc_ref[:, :middle] + early_ref[...].astype(F32)
    sum_ref[:, middle:] = acc_ref[:, middle:] + late_ref[...].astype(F32)
    samples = out_refs[0].shape[-1]

    def early_components():
        spans = spans_of(sum_ref.shape[-1], storing(sum_ref))
        collect(comps, rows, range(comps - 1), cross_ref, [sum_ref], work_refs, spans)

    multiply(0, rows, length, tpl_ref, cross_ref, work_refs, early_components)
    tm_index = lax.axis_index("tm")

    def storing_in(ref):
        def store(chunk):
            ref[:, :samples] = chunk.astype(ref.dtype)
            if ref.shape[1] > samples:
                ref[:, samples:] = jnp.zeros((rows, ref.shape[1] - samples), ref.dtype)

        return store

    spans = [
        (pl.multiple_of((tm_index ^ offset) * samples, LANES), samples, storing_in(ref))
        for offset, ref in enumerate(out_refs)
    ]
    collect(comps, rows, [comps - 1], cross_ref, [sum_ref], work_refs, spans)


def work_buffers(comps, rows, total, width, length):
    splits = -(-length // (2 * LANES))
    reach = total + (splits - 1) * 2 * LANES
    return [pltpu.VMEM((comps, LANES, width), BF16), pltpu.VMEM((comps, splits * rows, reach), F32)]


def first(rows, length, halo, crossing, tpl, shards, tails):
    chips, comps, samples = shards[0].shape
    total = samples * len(shards)
    width = total + up(length, LANES)
    count = chips * comps
    return pl.pallas_call(
        functools.partial(first_kernel, len(shards), chips, rows, length, halo, crossing),
        out_shape=[
            jax.ShapeDtypeStruct((count, width), F32),
            jax.ShapeDtypeStruct((count, total), F32),
            jax.ShapeDtypeStruct((2 * comps, width), F32),
            jax.ShapeDtypeStruct((rows, total), F32),
        ],
        in_specs=[VMEM] * (1 + len(shards) + chips),
        out_specs=[VMEM] * 4,
        scratch_shapes=[pltpu.VMEM((up(2 * count, 8), width), F32)]
        + work_buffers(comps, rows, total, width, length),
        compiler_params=params(24),
        cost_estimate=CHEAP,
    )(tpl, *shards, *tails)


def later(kernel, rows, total, length, out_shape, inputs, scratch=(), flops=1):
    comps, width = inputs[0].shape[0], inputs[1].shape[-1]
    return pl.pallas_call(
        kernel,
        out_shape=out_shape,
        in_specs=[VMEM] * len(inputs),
        out_specs=[VMEM] * len(out_shape),
        scratch_shapes=list(scratch) + work_buffers(comps, rows, total, width, length),
        compiler_params=params(24),
        cost_estimate=pl.CostEstimate(flops=flops, bytes_accessed=1, transcendentals=0),
    )(*inputs)


def gather_kernel(*refs):
    *part_refs, out_ref, held_ref, left = refs
    tm_index = lax.axis_index("tm")
    copies = []
    for offset, ref in enumerate(part_refs):
        held_ref[offset] = ref[:, : out_ref.shape[2]].astype(F32)
        copies.append(
            pltpu.make_async_copy(held_ref.at[offset], out_ref.at[tm_index ^ offset], left.at[offset])
        )
        copies[-1].start()
    for copy in copies:
        copy.wait()


def gather(parts):
    shape = (len(parts),) + parts[0].shape
    return pl.pallas_call(
        gather_kernel,
        out_shape=jax.ShapeDtypeStruct(shape, F32),
        in_specs=[VMEM] * len(parts),
        out_specs=HBM,
        scratch_shapes=[pltpu.VMEM(shape, F32), pltpu.SemaphoreType.DMA((len(parts),))],
        compiler_params=params(16),
    )(*parts)


def per_device(templates, channel_mask, waveforms, waveform_tail):
    length = templates.shape[-1]
    samples = waveforms.shape[-1]
    halo = waveform_tail.shape[-1]
    tm_count = lax.axis_size("tm")
    chips = lax.axis_size("sta") // 2
    tpl = jnp.transpose(templates[0, :, 0], (1, 2, 0))
    mask = channel_mask[..., 0]
    rows = tpl.shape[-1] // chips
    own = rows // 2
    total = samples * tm_count
    comps = tpl.shape[0]
    final = chips // 2
    between = [1] + [offset for offset in range(chips - 1, 1, -1) if offset != final]

    wave, tpl, mask = join(waveforms[0], waveform_tail[0], tpl, mask)
    waves = [wave] + [swap_with(wave, "sta", 2 * offset) for offset in range(1, chips)]
    offsets = [0] + between
    targets = [(offset, None) for offset in offsets] + [(final, 0), (final, 1)]
    messages = pack(targets, [rows] * len(offsets) + [own] * 2, tpl, mask)
    pieces = {offset: swap_with(messages[1 + i], "sta", 2 * offset) for i, offset in enumerate(between)}
    stacked = jnp.stack([part[:, :samples] for part in waves])
    shards = [stacked] + [swap_with(stacked, "tm", offset) for offset in range(1, tm_count)]
    late = [None, None]
    late[0], shards[-1] = lax.optimization_barrier((messages[-2], shards[-1]))
    late[1], shards[-2] = lax.optimization_barrier((messages[-1], shards[-2]))
    straight = swap_with(late[0], "sta", 2 * final)
    ext, inv, cross, acc = first(rows, length, halo, final, messages[0], shards, waves)
    latest, acc = lax.optimization_barrier((late[1], acc))
    crossed = swap_with(latest, "sta", 2 * final + 1)
    cross = swap_with(cross, "sta", 1)
    whole = jax.ShapeDtypeStruct((rows, total), F32)
    for offset in between[:-1]:
        kernel = functools.partial(middle_kernel, offset * comps, rows, length)
        (acc,) = later(kernel, rows, total, length, [whole], [pieces[offset], ext, inv, acc], flops=F_MID)
    middle = up(total // 2, LANES)
    half = jax.ShapeDtypeStruct((own, total), F32)
    halves = [jax.ShapeDtypeStruct((own, size), BF16) for size in (middle, total - middle)]
    kernel = functools.partial(parting_kernel, between[-1] * comps, rows, length)
    inputs = [pieces[between[-1]], ext, inv, acc]
    keep, *send = later(kernel, rows, total, length, [half] + halves, inputs, flops=F_PART)
    came = [swap_with(part, "sta", 1) for part in send]
    kernel = functools.partial(middle_kernel, final * comps, own, length)
    (acc,) = later(kernel, own, total, length, [half], [straight, ext, inv, keep], flops=F_JOIN)
    kernel = functools.partial(closing_kernel, tm_count, own, length)
    parts = [jax.ShapeDtypeStruct((own, samples), F32)] + [
        jax.ShapeDtypeStruct((own, samples + (EXTRA if offset & (offset - 1) else 0)), BF16)
        for offset in range(1, tm_count)
    ]
    inputs = [crossed, cross, acc, *came]
    parts = later(kernel, own, total, length, parts, inputs, [pltpu.VMEM((own, total), F32)], F_CLOSE)
    parts = [parts[0]] + [swap_with(parts[offset], "tm", offset) for offset in range(1, tm_count)]
    return gather(parts)


def solution(mesh):
    placed = (
        P("tm", None, "sta", None, None),
        P("tm", None, "sta"),
        P("sta", None, "tm"),
        P("sta", None, None),
    )
    return jax.shard_map(
        per_device, mesh=mesh, in_specs=placed, out_specs=P(None, "sta", "tm"), check_vma=False
    )
```

```python
import functools
import jax
import jax.numpy as jnp
from jax import lax
from jax.experimental import pallas as pl
from jax.experimental.pallas import tpu as pltpu
from jax.sharding import PartitionSpec as P

F32 = jnp.float32
BF16 = jnp.bfloat16
LANES = 128
CHUNK = 512
EXTRA = 128
VMEM = pl.BlockSpec(memory_space=pltpu.VMEM)
HBM = pl.BlockSpec(memory_space=pltpu.HBM)
F_MID, F_PART, F_JOIN, F_CLOSE = 500000000, 1, 500000000, 1
CHEAP = pl.CostEstimate(flops=1, bytes_accessed=1, transcendentals=0)


def params(limit_mib):
    return pltpu.CompilerParams(vmem_limit_bytes=limit_mib << 20)


def up(value, multiple):
    return (value + multiple - 1) // multiple * multiple


def swap_with(x, axis, offset):
    size = lax.axis_size(axis)
    return lax.ppermute(x, axis, [(i, i ^ offset) for i in range(size)])


def join_kernel(wave_ref, tail_ref, tpl_ref, mask_ref, out_ref, tpl_out, mask_out, wave_held, tail_held, arrived):
    pairs = [(wave_ref, wave_held), (tail_ref, tail_held), (mask_ref, mask_out)]
    pairs += [(tpl_ref.at[comp], tpl_out.at[comp]) for comp in range(tpl_ref.shape[0])]
    copies = [pltpu.make_async_copy(source, held, arrived.at[i]) for i, (source, held) in enumerate(pairs)]
    for copy in copies:
        copy.start()
    copies[0].wait()
    copies[1].wait()
    samples = wave_held.shape[-1]
    out_ref[...] = jnp.zeros_like(out_ref)
    out_ref[:, :samples] = wave_held[...]
    out_ref[:, samples : samples + tail_held.shape[-1]] = tail_held[...]
    for copy in copies[2:]:
        copy.wait()


def join(wave, tail, tpl, mask):
    inputs = (wave, tail, tpl, mask)
    return pl.pallas_call(
        join_kernel,
        out_shape=[
            jax.ShapeDtypeStruct((wave.shape[0], up(wave.shape[-1] + tail.shape[-1], LANES)), BF16),
            jax.ShapeDtypeStruct(tpl.shape, tpl.dtype),
            jax.ShapeDtypeStruct(mask.shape, mask.dtype),
        ],
        in_specs=[HBM] * 4,
        out_specs=[VMEM] * 3,
        scratch_shapes=[pltpu.VMEM(x.shape, x.dtype) for x in (wave, tail)] + [pltpu.SemaphoreType.DMA((3 + tpl.shape[0],))],
        compiler_params=params(16),
        cost_estimate=CHEAP,
    )(*[pltpu.with_memory_space_constraint(x, pltpu.HBM) for x in inputs])


def first_row(chip_offset, core_offset, all_rows):
    index = lax.axis_index("sta")
    rows = all_rows // (lax.axis_size("sta") // 2)
    row = (index // 2 ^ chip_offset) * rows
    return row if core_offset is None else row + (index % 2 ^ core_offset) * (rows // 2)


def fold_lags(rows, length):
    return up(-(-length // (LANES // rows)), 8)


def pack_kernel(targets, counts, length, tpl_ref, mask_ref, *tpl_outs):
    lane = lax.broadcasted_iota(jnp.int32, (1, LANES), 1)
    for target, rows, out_ref in zip(targets, counts, tpl_outs):
        lags = fold_lags(rows, length)
        row = first_row(*target, tpl_ref.shape[-1])
        tile = pl.multiple_of(row // LANES * LANES, LANES)
        mask = mask_ref[:, pl.ds(tile, LANES)].astype(F32)
        for comp in range(tpl_ref.shape[0]):
            values = tpl_ref[comp, :, pl.ds(tile, LANES)].astype(F32) * mask
            folded = jnp.zeros((lags, LANES), F32)
            for fold in range(LANES // rows):
                piece = values[fold * lags : min((fold + 1) * lags, length)]
                if piece.shape[0] == 0:
                    continue
                if piece.shape[0] < lags:
                    piece = jnp.concatenate([piece, jnp.zeros((lags - piece.shape[0], LANES), F32)], axis=0)
                turned = pltpu.roll(piece, (fold * rows - row % LANES + LANES) % LANES, 1)
                here = (lane >= fold * rows) & (lane < (fold + 1) * rows)
                folded = jnp.where(here, turned, folded)
            out_ref[comp] = folded.astype(BF16)


def pack(targets, counts, tpl, mask):
    comps, length, _ = tpl.shape
    return pl.pallas_call(
        functools.partial(pack_kernel, targets, counts, length),
        out_shape=[jax.ShapeDtypeStruct((comps, fold_lags(rows, length), LANES), BF16) for rows in counts],
        in_specs=[VMEM] * 2,
        out_specs=[VMEM] * len(counts),
        compiler_params=params(16),
        cost_estimate=CHEAP,
    )(tpl, mask)


def fill_samples(halo, tm_index, shard_refs, tail_refs, ext_ref):
    chips, comps, samples = shard_refs[0].shape
    total = samples * len(shard_refs)
    ext_ref[...] = jnp.zeros_like(ext_ref)
    for chip in range(chips):
        at = chip * comps
        for offset, ref in enumerate(shard_refs):
            start = pl.multiple_of((tm_index ^ offset) * samples, LANES)
            ext_ref[at : at + comps, pl.ds(start, samples)] = ref[chip].astype(F32)
        ext_ref[at : at + comps, total : total + halo] = tail_refs[chip][:, samples : samples + halo].astype(F32)


def fill_inverse(length, ext_ref, both_ref, inv_ref):
    count, width = ext_ref.shape
    total = inv_ref.shape[-1]
    both_ref[:count, :] = ext_ref[...]
    both_ref[count : 2 * count, :] = ext_ref[...] * ext_ref[...]
    result, done, span, doubled = None, 0, 1, both_ref[: 2 * count, :]
    while span <= length:
        if length & span:
            part = doubled if done == 0 else pltpu.roll(doubled, width - done, 1)
            result = part if result is None else result + part
            done += span
        span *= 2
        if span <= length:
            doubled = doubled + pltpu.roll(doubled, width - span // 2, 1)
    both_ref[: 2 * count, :] = result
    window_sum = both_ref[:count, :total]
    window_square = both_ref[count : 2 * count, :total]
    inv_ref[...] = lax.rsqrt(window_square - window_sum * window_sum / length + 1e-05)


def lag_rows(values, rows, length):
    lags = values.shape[0]
    folds = LANES // rows
    splits = -(-length // (2 * LANES))

    def over_folds(total):
        span = rows
        while span < LANES:
            total = total + pltpu.roll(total, span, 1)
            span *= 2
        return total

    lane = lax.broadcasted_iota(jnp.int32, values.shape, 1)
    lag = lax.broadcasted_iota(jnp.int32, values.shape, 0) + lane // rows * lags
    mean = over_folds(jnp.sum(values, axis=0, keepdims=True)) / length
    centred = jnp.where(lag < length, values - mean, 0.0)
    energy = over_folds(jnp.sum(centred * centred, axis=0, keepdims=True))
    weighted = centred * lax.rsqrt(energy + 1e-05)
    parts = [weighted] + [pltpu.roll(weighted, LANES - fold * rows, 1) for fold in range(1, folds)]
    wanted = splits * 2 * LANES
    if folds * lags < wanted:
        parts.append(jnp.zeros((wanted - folds * lags, LANES), F32))
    spread = jnp.concatenate(parts, axis=0)
    low = lax.broadcasted_iota(jnp.int32, (LANES, LANES), 1) < LANES // 2
    flip = (
        lax.broadcasted_iota(jnp.int32, (LANES, LANES), 0)
        + lax.broadcasted_iota(jnp.int32, (LANES, LANES), 1)
        == LANES - 1
    ).astype(BF16)
    result = []
    for split in range(splits):
        at = split * 2 * LANES
        both = jnp.where(low, spread[at : at + LANES], pltpu.roll(spread[at + LANES : at + 2 * LANES], LANES // 2, 1))
        turned = lax.dot_general(
            both.astype(BF16), flip, (((0,), (0,)), ((), ())), preferred_element_type=F32
        )
        result.append(jnp.concatenate([turned[:rows], turned[LANES // 2 : LANES // 2 + rows]], axis=1))
    return jnp.concatenate(result, axis=0).astype(BF16)


def fill_hankel(row, out_ref):
    width = row.shape[-1]
    spread = jnp.broadcast_to(row.astype(BF16), (LANES, width))
    out_ref[...] = pltpu.roll(spread, width - (LANES - 1), 1, stride=1, stride_axis=0)


def multiply(ext_at, rows, length, tpl_ref, ext_ref, work_refs, between=None):
    hankel_ref, product_ref = work_refs
    reach = product_ref.shape[-1]
    comps = tpl_ref.shape[0]
    for comp in range(comps):
        fill_hankel(ext_ref[ext_at + comp : ext_at + comp + 1, :], hankel_ref.at[comp])
    lhs = [lag_rows(tpl_ref[comp].astype(F32), rows, length) for comp in range(comps)]
    for comp in range(comps):
        if comp == comps - 1 and between is not None:
            between()
        rhs = jnp.concatenate(
            [hankel_ref[comp, :, :reach], hankel_ref[comp, :, LANES : LANES + reach]], axis=0
        )
        product_ref[comp] = jnp.dot(lhs[comp], rhs, preferred_element_type=F32)


def collect(inv_at, rows, comps, inv_ref, acc_refs, work_refs, spans):
    product_ref = work_refs[1]
    splits = product_ref.shape[1] // rows
    for start, size, store in spans:
        chunk = None
        for ref in acc_refs:
            part = ref[:, pl.ds(start, size)]
            chunk = part if chunk is None else chunk + part
        for comp in comps:
            part = product_ref[comp, :rows, pl.ds(start, size)]
            for split in range(1, splits):
                shift = split * 2 * LANES
                part = part + product_ref[comp, split * rows : (split + 1) * rows, pl.ds(start + shift, size)]
            part = part * inv_ref[inv_at + comp : inv_at + comp + 1, pl.ds(start, size)]
            chunk = part if chunk is None else chunk + part
        store(chunk)


def spans_of(total, store):
    return [
        (start, min(CHUNK, total - start), functools.partial(store, start)) for start in range(0, total, CHUNK)
    ]


def storing(ref):
    def store(start, chunk):
        ref[:, start : start + chunk.shape[1]] = chunk

    return store


def correlate(at, rows, length, tpl_ref, ext_ref, inv_ref, acc_refs, work_refs, store):
    multiply(at, rows, length, tpl_ref, ext_ref, work_refs)
    spans = spans_of(inv_ref.shape[-1], store)
    collect(at, rows, range(tpl_ref.shape[0]), inv_ref, acc_refs, work_refs, spans)


def first_kernel(shards, chips, rows, length, halo, crossing, tpl_ref, *refs):
    shard_refs, tail_refs = refs[:shards], refs[shards : shards + chips]
    ext_ref, inv_ref, cross_ref, sum_ref, both_ref, *work_refs = refs[shards + chips :]
    comps, total = tpl_ref.shape[0], inv_ref.shape[-1]
    fill_samples(halo, lax.axis_index("tm"), shard_refs, tail_refs, ext_ref)
    multiply(0, rows, length, tpl_ref, ext_ref, work_refs)
    fill_inverse(length, ext_ref, both_ref, inv_ref)
    cross_ref[:comps, :] = ext_ref[crossing * comps : (crossing + 1) * comps, :]
    cross_ref[comps:, :total] = inv_ref[crossing * comps : (crossing + 1) * comps, :]
    cross_ref[comps:, total:] = jnp.zeros((comps, cross_ref.shape[-1] - total), F32)
    collect(0, rows, range(comps), inv_ref, [], work_refs, spans_of(total, storing(sum_ref)))


def middle_kernel(at, rows, length, tpl_ref, ext_ref, inv_ref, acc_ref, sum_ref, *work_refs):
    correlate(at, rows, length, tpl_ref, ext_ref, inv_ref, [acc_ref], work_refs, storing(sum_ref))


def parting_kernel(at, rows, length, tpl_ref, ext_ref, inv_ref, acc_ref, keep_ref, early_ref, late_ref, *work_refs):
    own = rows // 2
    low = lax.axis_index("sta") % 2 == 0
    middle = early_ref.shape[-1]

    def store(start, chunk):
        stop = start + chunk.shape[1]
        keep_ref[:, start:stop] = jnp.where(low, chunk[:own], chunk[own:])
        send = jnp.where(low, chunk[own:], chunk[:own]).astype(BF16)
        if start < middle:
            early_ref[:, start : min(stop, middle)] = send[:, : min(stop, middle) - start]
        if stop > middle:
            late_ref[:, max(start, middle) - middle : stop - middle] = send[:, max(start, middle) - start :]

    correlate(at, rows, length, tpl_ref, ext_ref, inv_ref, [acc_ref], work_refs, store)


def closing_kernel(shards, rows, length, tpl_ref, cross_ref, acc_ref, early_ref, late_ref, *refs):
    out_refs, (sum_ref, *work_refs) = refs[:shards], refs[shards:]
    comps, middle = tpl_ref.shape[0], early_ref.shape[-1]
    sum_ref[:, :middle] = acc_ref[:, :middle] + early_ref[...].astype(F32)
    sum_ref[:, middle:] = acc_ref[:, middle:] + late_ref[...].astype(F32)
    samples = out_refs[0].shape[-1]

    def early_components():
        spans = spans_of(sum_ref.shape[-1], storing(sum_ref))
        collect(comps, rows, range(comps - 1), cross_ref, [sum_ref], work_refs, spans)

    multiply(0, rows, length, tpl_ref, cross_ref, work_refs, early_components)
    tm_index = lax.axis_index("tm")

    def storing_in(ref):
        def store(chunk):
            ref[:, :samples] = chunk.astype(ref.dtype)
            if ref.shape[1] > samples:
                ref[:, samples:] = jnp.zeros((rows, ref.shape[1] - samples), ref.dtype)

        return store

    spans = [
        (pl.multiple_of((tm_index ^ offset) * samples, LANES), samples, storing_in(ref))
        for offset, ref in enumerate(out_refs)
    ]
    collect(comps, rows, [comps - 1], cross_ref, [sum_ref], work_refs, spans)


def work_buffers(comps, rows, total, width, length):
    splits = -(-length // (2 * LANES))
    reach = total + (splits - 1) * 2 * LANES
    return [pltpu.VMEM((comps, LANES, width), BF16), pltpu.VMEM((comps, splits * rows, reach), F32)]


def first(rows, length, halo, crossing, tpl, shards, tails):
    chips, comps, samples = shards[0].shape
    total = samples * len(shards)
    width = total + up(length, LANES)
    count = chips * comps
    return pl.pallas_call(
        functools.partial(first_kernel, len(shards), chips, rows, length, halo, crossing),
        out_shape=[
            jax.ShapeDtypeStruct((count, width), F32),
            jax.ShapeDtypeStruct((count, total), F32),
            jax.ShapeDtypeStruct((2 * comps, width), F32),
            jax.ShapeDtypeStruct((rows, total), F32),
        ],
        in_specs=[VMEM] * (1 + len(shards) + chips),
        out_specs=[VMEM] * 4,
        scratch_shapes=[pltpu.VMEM((up(2 * count, 8), width), F32)]
        + work_buffers(comps, rows, total, width, length),
        compiler_params=params(24),
        cost_estimate=CHEAP,
    )(tpl, *shards, *tails)


def later(kernel, rows, total, length, out_shape, inputs, scratch=(), flops=1):
    comps, width = inputs[0].shape[0], inputs[1].shape[-1]
    return pl.pallas_call(
        kernel,
        out_shape=out_shape,
        in_specs=[VMEM] * len(inputs),
        out_specs=[VMEM] * len(out_shape),
        scratch_shapes=list(scratch) + work_buffers(comps, rows, total, width, length),
        compiler_params=params(24),
        cost_estimate=pl.CostEstimate(flops=flops, bytes_accessed=1, transcendentals=0),
    )(*inputs)


def gather_kernel(*refs):
    *part_refs, out_ref, held_ref, left = refs
    tm_index = lax.axis_index("tm")
    copies = []
    for offset, ref in enumerate(part_refs):
        held_ref[offset] = ref[:, : out_ref.shape[2]].astype(F32)
        copies.append(
            pltpu.make_async_copy(held_ref.at[offset], out_ref.at[tm_index ^ offset], left.at[offset])
        )
        copies[-1].start()
    for copy in copies:
        copy.wait()


def gather(parts):
    shape = (len(parts),) + parts[0].shape
    return pl.pallas_call(
        gather_kernel,
        out_shape=jax.ShapeDtypeStruct(shape, F32),
        in_specs=[VMEM] * len(parts),
        out_specs=HBM,
        scratch_shapes=[pltpu.VMEM(shape, F32), pltpu.SemaphoreType.DMA((len(parts),))],
        compiler_params=params(16),
    )(*parts)


def per_device(templates, channel_mask, waveforms, waveform_tail):
    length = templates.shape[-1]
    samples = waveforms.shape[-1]
    halo = waveform_tail.shape[-1]
    tm_count = lax.axis_size("tm")
    chips = lax.axis_size("sta") // 2
    tpl = jnp.transpose(templates[0, :, 0], (1, 2, 0))
    mask = channel_mask[..., 0]
    rows = tpl.shape[-1] // chips
    own = rows // 2
    total = samples * tm_count
    comps = tpl.shape[0]
    final = chips // 2
    between = [1] + [offset for offset in range(chips - 1, 1, -1) if offset != final]

    wave, tpl, mask = join(waveforms[0], waveform_tail[0], tpl, mask)
    waves = [wave] + [swap_with(wave, "sta", 2 * offset) for offset in range(1, chips)]
    offsets = [0] + between
    targets = [(offset, None) for offset in offsets] + [(final, 0), (final, 1)]
    messages = pack(targets, [rows] * len(offsets) + [own] * 2, tpl, mask)
    pieces = {offset: swap_with(messages[1 + i], "sta", 2 * offset) for i, offset in enumerate(between)}
    stacked = jnp.stack([part[:, :samples] for part in waves])
    shards = [stacked] + [swap_with(stacked, "tm", offset) for offset in range(1, tm_count)]
    late = [None, None]
    late[0], shards[-1] = lax.optimization_barrier((messages[-2], shards[-1]))
    late[1], shards[-2] = lax.optimization_barrier((messages[-1], shards[-2]))
    straight = swap_with(late[0], "sta", 2 * final)
    ext, inv, cross, acc = first(rows, length, halo, final, messages[0], shards, waves)
    latest, acc = lax.optimization_barrier((late[1], acc))
    crossed = swap_with(latest, "sta", 2 * final + 1)
    cross = swap_with(cross, "sta", 1)
    whole = jax.ShapeDtypeStruct((rows, total), F32)
    for offset in between[:-1]:
        kernel = functools.partial(middle_kernel, offset * comps, rows, length)
        (acc,) = later(kernel, rows, total, length, [whole], [pieces[offset], ext, inv, acc], flops=F_MID)
    middle = up(total // 2, LANES)
    half = jax.ShapeDtypeStruct((own, total), F32)
    halves = [jax.ShapeDtypeStruct((own, size), BF16) for size in (middle, total - middle)]
    kernel = functools.partial(parting_kernel, between[-1] * comps, rows, length)
    inputs = [pieces[between[-1]], ext, inv, acc]
    keep, *send = later(kernel, rows, total, length, [half] + halves, inputs, flops=F_PART)
    came = [swap_with(part, "sta", 1) for part in send]
    kernel = functools.partial(middle_kernel, final * comps, own, length)
    (acc,) = later(kernel, own, total, length, [half], [straight, ext, inv, keep], flops=F_JOIN)
    kernel = functools.partial(closing_kernel, tm_count, own, length)
    parts = [jax.ShapeDtypeStruct((own, samples), F32)] + [
        jax.ShapeDtypeStruct((own, samples + (EXTRA if offset & (offset - 1) else 0)), BF16)
        for offset in range(1, tm_count)
    ]
    inputs = [crossed, cross, acc, *came]
    parts = later(kernel, own, total, length, parts, inputs, [pltpu.VMEM((own, total), F32)], F_CLOSE)
    parts = [parts[0]] + [swap_with(parts[offset], "tm", offset) for offset in range(1, tm_count)]
    return gather(parts)


def solution(mesh):
    placed = (
        P("tm", None, "sta", None, None),
        P("tm", None, "sta"),
        P("sta", None, "tm"),
        P("sta", None, None),
    )
    return jax.shard_map(
        per_device, mesh=mesh, in_specs=placed, out_specs=P(None, "sta", "tm"), check_vma=False
    )
```

```python
import functools
import jax
import jax.numpy as jnp
from jax import lax
from jax.experimental import pallas as pl
from jax.experimental.pallas import tpu as pltpu
from jax.sharding import PartitionSpec as P

F32 = jnp.float32
BF16 = jnp.bfloat16
LANES = 128
CHUNK = 512
EXTRA = 128
VMEM = pl.BlockSpec(memory_space=pltpu.VMEM)
HBM = pl.BlockSpec(memory_space=pltpu.HBM)
F_MID, F_PART, F_JOIN, F_CLOSE = 500000000, 1, 500000000, 1
CHEAP = pl.CostEstimate(flops=1, bytes_accessed=1, transcendentals=0)


def params(limit_mib):
    return pltpu.CompilerParams(vmem_limit_bytes=limit_mib << 20)


def up(value, multiple):
    return (value + multiple - 1) // multiple * multiple


def swap_with(x, axis, offset):
    size = lax.axis_size(axis)
    return lax.ppermute(x, axis, [(i, i ^ offset) for i in range(size)])


def join_kernel(wave_ref, tail_ref, tpl_ref, mask_ref, out_ref, tpl_out, mask_out, wave_held, tail_held, arrived):
    pairs = [(wave_ref, wave_held), (tail_ref, tail_held), (mask_ref, mask_out)]
    pairs += [(tpl_ref.at[comp], tpl_out.at[comp]) for comp in range(tpl_ref.shape[0])]
    copies = [pltpu.make_async_copy(source, held, arrived.at[i]) for i, (source, held) in enumerate(pairs)]
    for copy in copies:
        copy.start()
    copies[0].wait()
    copies[1].wait()
    samples = wave_held.shape[-1]
    out_ref[...] = jnp.zeros_like(out_ref)
    out_ref[:, :samples] = wave_held[...]
    out_ref[:, samples : samples + tail_held.shape[-1]] = tail_held[...]
    for copy in copies[2:]:
        copy.wait()


def join(wave, tail, tpl, mask):
    inputs = (wave, tail, tpl, mask)
    return pl.pallas_call(
        join_kernel,
        out_shape=[
            jax.ShapeDtypeStruct((wave.shape[0], up(wave.shape[-1] + tail.shape[-1], LANES)), BF16),
            jax.ShapeDtypeStruct(tpl.shape, tpl.dtype),
            jax.ShapeDtypeStruct(mask.shape, mask.dtype),
        ],
        in_specs=[HBM] * 4,
        out_specs=[VMEM] * 3,
        scratch_shapes=[pltpu.VMEM(x.shape, x.dtype) for x in (wave, tail)] + [pltpu.SemaphoreType.DMA((3 + tpl.shape[0],))],
        compiler_params=params(16),
        cost_estimate=CHEAP,
    )(*[pltpu.with_memory_space_constraint(x, pltpu.HBM) for x in inputs])


def first_row(chip_offset, core_offset, all_rows):
    index = lax.axis_index("sta")
    rows = all_rows // (lax.axis_size("sta") // 2)
    row = (index // 2 ^ chip_offset) * rows
    return row if core_offset is None else row + (index % 2 ^ core_offset) * (rows // 2)


def fold_lags(rows, length):
    return up(-(-length // (LANES // rows)), 8)


def pack_kernel(targets, counts, length, tpl_ref, mask_ref, *tpl_outs):
    lane = lax.broadcasted_iota(jnp.int32, (1, LANES), 1)
    for target, rows, out_ref in zip(targets, counts, tpl_outs):
        lags = fold_lags(rows, length)
        row = first_row(*target, tpl_ref.shape[-1])
        tile = pl.multiple_of(row // LANES * LANES, LANES)
        mask = mask_ref[:, pl.ds(tile, LANES)].astype(F32)
        for comp in range(tpl_ref.shape[0]):
            values = tpl_ref[comp, :, pl.ds(tile, LANES)].astype(F32) * mask
            folded = jnp.zeros((lags, LANES), F32)
            for fold in range(LANES // rows):
                piece = values[fold * lags : min((fold + 1) * lags, length)]
                if piece.shape[0] == 0:
                    continue
                if piece.shape[0] < lags:
                    piece = jnp.concatenate([piece, jnp.zeros((lags - piece.shape[0], LANES), F32)], axis=0)
                turned = pltpu.roll(piece, (fold * rows - row % LANES + LANES) % LANES, 1)
                here = (lane >= fold * rows) & (lane < (fold + 1) * rows)
                folded = jnp.where(here, turned, folded)
            out_ref[comp] = folded.astype(BF16)


def pack(targets, counts, tpl, mask):
    comps, length, _ = tpl.shape
    return pl.pallas_call(
        functools.partial(pack_kernel, targets, counts, length),
        out_shape=[jax.ShapeDtypeStruct((comps, fold_lags(rows, length), LANES), BF16) for rows in counts],
        in_specs=[VMEM] * 2,
        out_specs=[VMEM] * len(counts),
        compiler_params=params(16),
        cost_estimate=CHEAP,
    )(tpl, mask)


def fill_samples(halo, tm_index, shard_refs, tail_refs, ext_ref):
    chips, comps, samples = shard_refs[0].shape
    total = samples * len(shard_refs)
    ext_ref[...] = jnp.zeros_like(ext_ref)
    for chip in range(chips):
        at = chip * comps
        for offset, ref in enumerate(shard_refs):
            start = pl.multiple_of((tm_index ^ offset) * samples, LANES)
            ext_ref[at : at + comps, pl.ds(start, samples)] = ref[chip].astype(F32)
        ext_ref[at : at + comps, total : total + halo] = tail_refs[chip][:, samples : samples + halo].astype(F32)


def fill_inverse(length, ext_ref, both_ref, inv_ref):
    count, width = ext_ref.shape
    total = inv_ref.shape[-1]
    both_ref[:count, :] = ext_ref[...]
    both_ref[count : 2 * count, :] = ext_ref[...] * ext_ref[...]
    result, done, span, doubled = None, 0, 1, both_ref[: 2 * count, :]
    while span <= length:
        if length & span:
            part = doubled if done == 0 else pltpu.roll(doubled, width - done, 1)
            result = part if result is None else result + part
            done += span
        span *= 2
        if span <= length:
            doubled = doubled + pltpu.roll(doubled, width - span // 2, 1)
    both_ref[: 2 * count, :] = result
    window_sum = both_ref[:count, :total]
    window_square = both_ref[count : 2 * count, :total]
    inv_ref[...] = lax.rsqrt(window_square - window_sum * window_sum / length + 1e-05)


def lag_rows(values, rows, length):
    lags = values.shape[0]
    folds = LANES // rows
    splits = -(-length // (2 * LANES))

    def over_folds(total):
        span = rows
        while span < LANES:
            total = total + pltpu.roll(total, span, 1)
            span *= 2
        return total

    lane = lax.broadcasted_iota(jnp.int32, values.shape, 1)
    lag = lax.broadcasted_iota(jnp.int32, values.shape, 0) + lane // rows * lags
    mean = over_folds(jnp.sum(values, axis=0, keepdims=True)) / length
    centred = jnp.where(lag < length, values - mean, 0.0)
    energy = over_folds(jnp.sum(centred * centred, axis=0, keepdims=True))
    weighted = centred * lax.rsqrt(energy + 1e-05)
    parts = [weighted] + [pltpu.roll(weighted, LANES - fold * rows, 1) for fold in range(1, folds)]
    wanted = splits * 2 * LANES
    if folds * lags < wanted:
        parts.append(jnp.zeros((wanted - folds * lags, LANES), F32))
    spread = jnp.concatenate(parts, axis=0)
    low = lax.broadcasted_iota(jnp.int32, (LANES, LANES), 1) < LANES // 2
    flip = (
        lax.broadcasted_iota(jnp.int32, (LANES, LANES), 0)
        + lax.broadcasted_iota(jnp.int32, (LANES, LANES), 1)
        == LANES - 1
    ).astype(BF16)
    result = []
    for split in range(splits):
        at = split * 2 * LANES
        both = jnp.where(low, spread[at : at + LANES], pltpu.roll(spread[at + LANES : at + 2 * LANES], LANES // 2, 1))
        turned = lax.dot_general(
            both.astype(BF16), flip, (((0,), (0,)), ((), ())), preferred_element_type=F32
        )
        result.append(jnp.concatenate([turned[:rows], turned[LANES // 2 : LANES // 2 + rows]], axis=1))
    return jnp.concatenate(result, axis=0).astype(BF16)


def fill_hankel(row, out_ref):
    width = row.shape[-1]
    spread = jnp.broadcast_to(row.astype(BF16), (LANES, width))
    out_ref[...] = pltpu.roll(spread, width - (LANES - 1), 1, stride=1, stride_axis=0)


def multiply(ext_at, rows, length, tpl_ref, ext_ref, work_refs, between=None):
    hankel_ref, product_ref = work_refs
    reach = product_ref.shape[-1]
    comps = tpl_ref.shape[0]
    for comp in range(comps):
        fill_hankel(ext_ref[ext_at + comp : ext_at + comp + 1, :], hankel_ref.at[comp])
    lhs = [lag_rows(tpl_ref[comp].astype(F32), rows, length) for comp in range(comps)]
    for comp in range(comps):
        if comp == comps - 1 and between is not None:
            between()
        rhs = jnp.concatenate(
            [hankel_ref[comp, :, :reach], hankel_ref[comp, :, LANES : LANES + reach]], axis=0
        )
        product_ref[comp] = jnp.dot(lhs[comp], rhs, preferred_element_type=F32)


def collect(inv_at, rows, comps, inv_ref, acc_refs, work_refs, spans):
    product_ref = work_refs[1]
    splits = product_ref.shape[1] // rows
    for start, size, store in spans:
        chunk = None
        for ref in acc_refs:
            part = ref[:, pl.ds(start, size)]
            chunk = part if chunk is None else chunk + part
        for comp in comps:
            part = product_ref[comp, :rows, pl.ds(start, size)]
            for split in range(1, splits):
                shift = split * 2 * LANES
                part = part + product_ref[comp, split * rows : (split + 1) * rows, pl.ds(start + shift, size)]
            part = part * inv_ref[inv_at + comp : inv_at + comp + 1, pl.ds(start, size)]
            chunk = part if chunk is None else chunk + part
        store(chunk)


def spans_of(total, store):
    return [
        (start, min(CHUNK, total - start), functools.partial(store, start)) for start in range(0, total, CHUNK)
    ]


def storing(ref):
    def store(start, chunk):
        ref[:, start : start + chunk.shape[1]] = chunk

    return store


def correlate(at, rows, length, tpl_ref, ext_ref, inv_ref, acc_refs, work_refs, store):
    multiply(at, rows, length, tpl_ref, ext_ref, work_refs)
    spans = spans_of(inv_ref.shape[-1], store)
    collect(at, rows, range(tpl_ref.shape[0]), inv_ref, acc_refs, work_refs, spans)


def first_kernel(shards, chips, rows, length, halo, crossing, tpl_ref, *refs):
    shard_refs, tail_refs = refs[:shards], refs[shards : shards + chips]
    ext_ref, inv_ref, cross_ref, sum_ref, both_ref, *work_refs = refs[shards + chips :]
    comps, total = tpl_ref.shape[0], inv_ref.shape[-1]
    fill_samples(halo, lax.axis_index("tm"), shard_refs, tail_refs, ext_ref)
    multiply(0, rows, length, tpl_ref, ext_ref, work_refs)
    fill_inverse(length, ext_ref, both_ref, inv_ref)
    cross_ref[:comps, :] = ext_ref[crossing * comps : (crossing + 1) * comps, :]
    cross_ref[comps:, :total] = inv_ref[crossing * comps : (crossing + 1) * comps, :]
    cross_ref[comps:, total:] = jnp.zeros((comps, cross_ref.shape[-1] - total), F32)
    collect(0, rows, range(comps), inv_ref, [], work_refs, spans_of(total, storing(sum_ref)))


def middle_kernel(at, rows, length, tpl_ref, ext_ref, inv_ref, acc_ref, sum_ref, *work_refs):
    correlate(at, rows, length, tpl_ref, ext_ref, inv_ref, [acc_ref], work_refs, storing(sum_ref))


def parting_kernel(at, rows, length, tpl_ref, ext_ref, inv_ref, acc_ref, keep_ref, early_ref, late_ref, *work_refs):
    own = rows // 2
    low = lax.axis_index("sta") % 2 == 0
    middle = early_ref.shape[-1]

    def store(start, chunk):
        stop = start + chunk.shape[1]
        keep_ref[:, start:stop] = jnp.where(low, chunk[:own], chunk[own:])
        send = jnp.where(low, chunk[own:], chunk[:own]).astype(BF16)
        if start < middle:
            early_ref[:, start : min(stop, middle)] = send[:, : min(stop, middle) - start]
        if stop > middle:
            late_ref[:, max(start, middle) - middle : stop - middle] = send[:, max(start, middle) - start :]

    correlate(at, rows, length, tpl_ref, ext_ref, inv_ref, [acc_ref], work_refs, store)


def closing_kernel(shards, rows, length, tpl_ref, cross_ref, acc_ref, early_ref, late_ref, *refs):
    out_refs, (sum_ref, *work_refs) = refs[:shards], refs[shards:]
    comps, middle = tpl_ref.shape[0], early_ref.shape[-1]
    sum_ref[:, :middle] = acc_ref[:, :middle] + early_ref[...].astype(F32)
    sum_ref[:, middle:] = acc_ref[:, middle:] + late_ref[...].astype(F32)
    samples = out_refs[0].shape[-1]

    def early_components():
        spans = spans_of(sum_ref.shape[-1], storing(sum_ref))
        collect(comps, rows, range(comps - 1), cross_ref, [sum_ref], work_refs, spans)

    multiply(0, rows, length, tpl_ref, cross_ref, work_refs, early_components)
    tm_index = lax.axis_index("tm")

    def storing_in(ref):
        def store(chunk):
            ref[:, :samples] = chunk.astype(ref.dtype)
            if ref.shape[1] > samples:
                ref[:, samples:] = jnp.zeros((rows, ref.shape[1] - samples), ref.dtype)

        return store

    spans = [
        (pl.multiple_of((tm_index ^ offset) * samples, LANES), samples, storing_in(ref))
        for offset, ref in enumerate(out_refs)
    ]
    collect(comps, rows, [comps - 1], cross_ref, [sum_ref], work_refs, spans)


def work_buffers(comps, rows, total, width, length):
    splits = -(-length // (2 * LANES))
    reach = total + (splits - 1) * 2 * LANES
    return [pltpu.VMEM((comps, LANES, width), BF16), pltpu.VMEM((comps, splits * rows, reach), F32)]


def first(rows, length, halo, crossing, tpl, shards, tails):
    chips, comps, samples = shards[0].shape
    total = samples * len(shards)
    width = total + up(length, LANES)
    count = chips * comps
    return pl.pallas_call(
        functools.partial(first_kernel, len(shards), chips, rows, length, halo, crossing),
        out_shape=[
            jax.ShapeDtypeStruct((count, width), F32),
            jax.ShapeDtypeStruct((count, total), F32),
            jax.ShapeDtypeStruct((2 * comps, width), F32),
            jax.ShapeDtypeStruct((rows, total), F32),
        ],
        in_specs=[VMEM] * (1 + len(shards) + chips),
        out_specs=[VMEM] * 4,
        scratch_shapes=[pltpu.VMEM((up(2 * count, 8), width), F32)]
        + work_buffers(comps, rows, total, width, length),
        compiler_params=params(24),
        cost_estimate=CHEAP,
    )(tpl, *shards, *tails)


def later(kernel, rows, total, length, out_shape, inputs, scratch=(), flops=1):
    comps, width = inputs[0].shape[0], inputs[1].shape[-1]
    return pl.pallas_call(
        kernel,
        out_shape=out_shape,
        in_specs=[VMEM] * len(inputs),
        out_specs=[VMEM] * len(out_shape),
        scratch_shapes=list(scratch) + work_buffers(comps, rows, total, width, length),
        compiler_params=params(24),
        cost_estimate=pl.CostEstimate(flops=flops, bytes_accessed=1, transcendentals=0),
    )(*inputs)


def gather_kernel(*refs):
    *part_refs, out_ref, held_ref, left = refs
    tm_index = lax.axis_index("tm")
    copies = []
    for offset, ref in enumerate(part_refs):
        held_ref[offset] = ref[:, : out_ref.shape[2]].astype(F32)
        copies.append(
            pltpu.make_async_copy(held_ref.at[offset], out_ref.at[tm_index ^ offset], left.at[offset])
        )
        copies[-1].start()
    for copy in copies:
        copy.wait()


def gather(parts):
    shape = (len(parts),) + parts[0].shape
    return pl.pallas_call(
        gather_kernel,
        out_shape=jax.ShapeDtypeStruct(shape, F32),
        in_specs=[VMEM] * len(parts),
        out_specs=HBM,
        scratch_shapes=[pltpu.VMEM(shape, F32), pltpu.SemaphoreType.DMA((len(parts),))],
        compiler_params=params(16),
    )(*parts)


def per_device(templates, channel_mask, waveforms, waveform_tail):
    length = templates.shape[-1]
    samples = waveforms.shape[-1]
    halo = waveform_tail.shape[-1]
    tm_count = lax.axis_size("tm")
    chips = lax.axis_size("sta") // 2
    tpl = jnp.transpose(templates[0, :, 0], (1, 2, 0))
    mask = channel_mask[..., 0]
    rows = tpl.shape[-1] // chips
    own = rows // 2
    total = samples * tm_count
    comps = tpl.shape[0]
    final = chips // 2
    between = [1] + [offset for offset in range(chips - 1, 1, -1) if offset != final]

    wave, tpl, mask = join(waveforms[0], waveform_tail[0], tpl, mask)
    waves = [wave] + [swap_with(wave, "sta", 2 * offset) for offset in range(1, chips)]
    offsets = [0] + between
    targets = [(offset, None) for offset in offsets] + [(final, 0), (final, 1)]
    messages = pack(targets[1:-2], [rows] * len(between), tpl, mask)
    rest = pack(targets[:1] + targets[-2:], [rows, own, own], tpl, mask)
    messages = [rest[0], *messages, *rest[1:]]
    pieces = {offset: swap_with(messages[1 + i], "sta", 2 * offset) for i, offset in enumerate(between)}
    stacked = jnp.stack([part[:, :samples] for part in waves])
    shards = [stacked] + [swap_with(stacked, "tm", offset) for offset in range(1, tm_count)]
    late = [None, None]
    late[0], shards[-1] = lax.optimization_barrier((messages[-2], shards[-1]))
    late[1], shards[-2] = lax.optimization_barrier((messages[-1], shards[-2]))
    straight = swap_with(late[0], "sta", 2 * final)
    ext, inv, cross, acc = first(rows, length, halo, final, messages[0], shards, waves)
    latest, acc = lax.optimization_barrier((late[1], acc))
    crossed = swap_with(latest, "sta", 2 * final + 1)
    cross = swap_with(cross, "sta", 1)
    whole = jax.ShapeDtypeStruct((rows, total), F32)
    for offset in between[:-1]:
        kernel = functools.partial(middle_kernel, offset * comps, rows, length)
        (acc,) = later(kernel, rows, total, length, [whole], [pieces[offset], ext, inv, acc], flops=F_MID)
    middle = up(total // 2, LANES)
    half = jax.ShapeDtypeStruct((own, total), F32)
    halves = [jax.ShapeDtypeStruct((own, size), BF16) for size in (middle, total - middle)]
    kernel = functools.partial(parting_kernel, between[-1] * comps, rows, length)
    inputs = [pieces[between[-1]], ext, inv, acc]
    keep, *send = later(kernel, rows, total, length, [half] + halves, inputs, flops=F_PART)
    came = [swap_with(part, "sta", 1) for part in send]
    kernel = functools.partial(middle_kernel, final * comps, own, length)
    (acc,) = later(kernel, own, total, length, [half], [straight, ext, inv, keep], flops=F_JOIN)
    kernel = functools.partial(closing_kernel, tm_count, own, length)
    parts = [jax.ShapeDtypeStruct((own, samples), F32)] + [
        jax.ShapeDtypeStruct((own, samples + (EXTRA if offset & (offset - 1) else 0)), BF16)
        for offset in range(1, tm_count)
    ]
    inputs = [crossed, cross, acc, *came]
    parts = later(kernel, own, total, length, parts, inputs, [pltpu.VMEM((own, total), F32)], F_CLOSE)
    parts = [parts[0]] + [swap_with(parts[offset], "tm", offset) for offset in range(1, tm_count)]
    return gather(parts)


def solution(mesh):
    placed = (
        P("tm", None, "sta", None, None),
        P("tm", None, "sta"),
        P("sta", None, "tm"),
        P("sta", None, None),
    )
    return jax.shard_map(
        per_device, mesh=mesh, in_specs=placed, out_specs=P(None, "sta", "tm"), check_vma=False
    )
```
